128 devices in a mesh: gx: 8 (over z, core), gy: 16 (over y, x).
Axes of the slice: x: 4, y: 4, z: 4, core: 2. Of those that a mesh axis runs over, the one named last changes fastest.
Arguments:
- charges: float32 [8192, 128], P(('gx', 'gy')), may hold values from -0.8 to 0.8
- positions: float32 [8192, 3, 128], P(('gx', 'gy')), may hold values from 0 to 1
- widths: float32 [8192, 128], P(('gx', 'gy')), may hold values from 0.05 to 0.5
- site_counts: int32 [8192], P(('gx', 'gy')), may hold values from 1 to 128, 786432 in all
- pair_records: int32 [32768, 3], P(('gx', 'gy')), may hold values from 0 to 127, as said below
Outputs:
- near_potential: float32 [8192, 128], P(('gx', 'gy'))
- far_potential: float32 [8192], P(('gx', 'gy'))
The draws below stay inside these ranges and needn't reach their ends.
Inputs may be any that keep to these rules, and one draw needn't show every extreme that they name: `pair_records`: rows k * 256 to (k + 1) * 256 - 1 are the pairs owned by device k. Each row names a home device and two different local boxes of that device's 4 x 4 x 4 block whose cells touch (differ by at most 1 in every coordinate). Among one owner's rows at most 8 name one home device, and some home device is named exactly 8 times by every owner.
All inputs are finite; a program needn't handle non-finite values. No bound on the sum of `site_counts` on one device may be relied on, other than what follows from the above.
Results may differ from the reference program's by a relative error of at most 0.0003.
Values sent between devices are 32-bit elements; how exact they have to be, the bound alone decides.
A program may use at most 64 MiB of HBM per device.

```python
import math
import jax
import jax.numpy as jnp
import numpy as np
from jax import lax

P_SIZE = 128
BOX_DEV = 64
CAP = 8
PAIR_DEV = 256
BOXES = 8192
N_GX = 8
N_GY = 16


def draw_pair_records(key, part):
    key = jax.random.fold_in(key, 7)
    key_weight, key_hot, key_jitter, key_first, key_offset = jax.random.split(key, 5)
    count_dev = N_GX * N_GY
    pool_size = count_dev * CAP
    home_weight = jax.random.randint(key_weight, (count_dev,), 0, 3)
    hot_device = jax.random.randint(key_hot, (), 0, count_dev)
    home_weight = jnp.where(jnp.arange(count_dev) == hot_device, 3, home_weight)
    slot_home = jnp.arange(pool_size) // CAP
    jitter_bits = jax.random.randint(key_jitter, (count_dev, pool_size), 0, 4096)
    slot_score = (home_weight[slot_home][None, :] * 4096 + jitter_bits) * pool_size + jnp.arange(pool_size)[None, :]
    _, chosen = lax.top_k(slot_score, PAIR_DEV)
    home_dev = chosen // CAP
    box_first = jax.random.randint(key_first, (count_dev, PAIR_DEV), 0, 64)
    step_offset = jax.random.randint(key_offset, (count_dev, PAIR_DEV, 3), -1, 2)
    all_zero = jnp.all(step_offset == 0, axis=-1)
    step_offset = step_offset.at[..., 2].set(jnp.where(all_zero, 1, step_offset[..., 2]))
    coords = jnp.stack([box_first // 16, box_first // 4 % 4, box_first % 4], axis=-1)
    shifted = coords + step_offset
    shifted = jnp.where((shifted < 0) | (shifted > 3), coords - step_offset, shifted)
    box_second = shifted[..., 0] * 16 + shifted[..., 1] * 4 + shifted[..., 2]
    return jnp.stack([home_dev, box_first, box_second], axis=-1).reshape(count_dev * PAIR_DEV, 3).astype(jnp.int32)


def block_levels(key, shape, shards, smallest, top_value):
    gain = 1.0
    for position, blocks in shards:
        steps = jax.random.uniform(jax.random.fold_in(jax.random.fold_in(key, 6), position), (blocks,), jnp.float32, smallest / len(shards), top_value / len(shards))
        gain = gain * jnp.repeat(jnp.exp(steps), shape[position] // blocks).reshape((-1,) + (1,) * (len(shape) - 1 - position))
    return gain


def profile(count, total, most, slope):
    portions = [(1 << 20) // math.isqrt(grade ** slope) + 1 for grade in range(2, count + 1)]
    spare, holding = total - most - (count - 1), [1] * (count - 1)
    while spare > 0:
        free = [i for i in range(count - 1) if holding[i] < most]
        whole, remaining = sum([portions[i] for i in free]), spare
        for i in free:
            more = min(most - holding[i], max(1, remaining * portions[i] // whole), spare)
            holding[i] = holding[i] + more
            spare = spare - more
    return np.array([most] + holding)


def ragged(own_key, number_of, total, limit, lean):
    if number_of == 2:
        one = jax.random.randint(own_key, (), max(1, total - limit), min(limit, total - 1) + 1)
        return jnp.stack([one, total - one])
    sizes = jnp.asarray(profile(number_of, total, limit, lean), jnp.int32)
    twos = (number_of - 1) // 2
    donor, sink = sizes[1:1 + 2 * twos:2], sizes[2:2 + 2 * twos:2]
    margin = jnp.minimum(donor - 1, limit - sink)
    moved = jax.random.randint(jax.random.fold_in(own_key, 1), (twos,), 0, 1 << 20) % (margin + 1)
    sizes = sizes.at[1:1 + 2 * twos:2].set(donor - moved).at[2:2 + 2 * twos:2].set(sink + moved)
    return sizes[jax.random.permutation(jax.random.fold_in(own_key, 2), number_of)]


def noise(rng, extent, scale, most, pieces=(), kind=jnp.bfloat16):
    loudness = block_levels(rng, extent, pieces, -0.22, 0.18) if pieces else 1.0
    entries = jax.random.normal(rng, extent, jnp.float32) * scale * loudness
    return jnp.minimum(jnp.maximum(entries, -most), most).astype(kind)


def setup_inputs(seed: int = 0) -> dict:
    key_list = jax.random.split(jax.random.key(seed), 6)
    charges = noise(key_list[0], (BOXES, P_SIZE), 0.1, 0.8, ((0, 128),), jnp.float32)
    positions = jnp.clip(1.0 * jax.random.uniform(key_list[1], (BOXES, 3, P_SIZE), jnp.float32) ** block_levels(key_list[1], (BOXES, 3, P_SIZE), ((0, 128),), -0.2, 0.2), 0.0, 1.0)
    widths = jnp.clip(jnp.exp(math.log(0.5) - 2.3025851 * jax.random.uniform(key_list[2], (BOXES, P_SIZE), jnp.float32) ** block_levels(key_list[2], (BOXES, P_SIZE), ((0, 128),), -0.2, 0.2)), 0.05, 0.5)
    site_counts = ragged(key_list[3], BOXES, BOXES * P_SIZE * 3 // 4, P_SIZE, 0).astype(jnp.int32)
    pair_records = draw_pair_records(jax.random.fold_in(key_list[5], 71), 0)
    return {"charges": charges, "positions": positions, "widths": widths, "site_counts": site_counts, "pair_records": pair_records}


SOFT_TERM = 2.0

def box_coords(box_index):
    return jnp.stack([box_index // 16, box_index // 4 % 4, box_index % 4], axis=-1).astype(jnp.float32)

def parent_local(local_box):
    return local_box // 32 * 4 + local_box // 8 % 2 * 2 + local_box % 4 // 2

def pair_terms(block_first, block_second, box_first, box_second):
    offset_box = box_coords(box_second) - box_coords(box_first)
    sites = block_first.shape[2]
    distance = jnp.zeros((block_first.shape[0], sites, sites), jnp.float32)
    for axis_number in range(3):
        delta_axis = offset_box[:, axis_number, None, None] + block_second[:, 1 + axis_number, None, :] - block_first[:, 1 + axis_number, :, None]
        distance = distance + delta_axis * delta_axis
    pair_width = block_first[:, 4, :, None] + block_second[:, 4, None, :]
    kernel = lax.rsqrt(distance + pair_width) - lax.rsqrt(distance + pair_width + SOFT_TERM)
    phi_first = jnp.einsum('nij,nj->ni', kernel, block_second[:, 0], precision=lax.Precision.HIGHEST)
    phi_second = jnp.einsum('nij,ni->nj', kernel, block_first[:, 0], precision=lax.Precision.HIGHEST)
    return (phi_first, phi_second)

def far_field(parent_charge, device_flat, local_box, count_gy):
    box_xyz = jnp.stack([4 * (device_flat // count_gy) + local_box // 16, 4 * (device_flat % count_gy) + local_box // 4 % 4, local_box % 4], axis=-1).astype(jnp.float32) + 0.5
    parent_all = jnp.arange(parent_charge.shape[0])
    parent_dev = parent_all // 8
    parent_own = parent_all % 8
    parent_xyz = jnp.stack([4 * (parent_dev // count_gy) + 2 * (parent_own // 4), 4 * (parent_dev % count_gy) + 2 * (parent_own // 2 % 2), 2 * (parent_own % 2)], axis=-1).astype(jnp.float32) + 1.0
    distance = jnp.zeros((box_xyz.shape[0], parent_xyz.shape[0]), jnp.float32)
    for axis_number in range(3):
        delta_axis = box_xyz[:, axis_number, None] - parent_xyz[None, :, axis_number]
        distance = distance + delta_axis * delta_axis
    return lax.optimization_barrier(jnp.sum(lax.rsqrt(distance + SOFT_TERM) * parent_charge[None, :], axis=1))

def reference(charges, positions, widths, site_counts, pair_records):
    count_dev = N_GX * N_GY
    site_live = jnp.arange(P_SIZE)[None, :] < site_counts[:, None]
    charge_live = jnp.where(site_live, charges, jnp.float32(0.0)).astype(jnp.float32)
    box_block = jnp.concatenate([charge_live[:, None, :], positions, widths[:, None, :]], axis=1)
    records = pair_records.reshape(count_dev, PAIR_DEV, 3)

    def accumulate(running, owner_rows):
        first_ids = owner_rows[:, 0] * BOX_DEV + owner_rows[:, 1]
        second_ids = owner_rows[:, 0] * BOX_DEV + owner_rows[:, 2]
        phi_first, phi_second = pair_terms(box_block[first_ids], box_block[second_ids], owner_rows[:, 1], owner_rows[:, 2])
        running = running.at[first_ids].add(phi_first).at[second_ids].add(phi_second)
        return (running, None)
    near, _ = lax.scan(accumulate, jnp.zeros((count_dev * BOX_DEV, P_SIZE), jnp.float32), records)
    near_potential = jnp.where(site_live, near, jnp.float32(0.0))
    box_charge = lax.optimization_barrier(jnp.sum(charge_live, axis=1))
    all_boxes = jnp.arange(count_dev * BOX_DEV)
    device_flat = all_boxes // BOX_DEV
    local_box = all_boxes % BOX_DEV
    parent_ids = device_flat * 8 + parent_local(local_box)
    parent_charge = jax.ops.segment_sum(box_charge, parent_ids, num_segments=count_dev * 8)
    far_potential = far_field(parent_charge, device_flat, local_box, N_GY)
    return (near_potential, far_potential)
```

```python
import jax
import jax.numpy as jnp
from jax import lax
from jax.experimental import pallas as pl
from jax.experimental.pallas import tpu as pltpu
from jax.sharding import PartitionSpec as P

F32, BF16, I32 = jnp.float32, jnp.bfloat16, jnp.int32
MESH = pl.DeviceIdType.MESH
GX, GY, CAP = 8, 16, 8
DEVICES = GX * GY
DEPTH = 48
SOFT_TERM = 2.0


def iota(shape, dim):
    return lax.broadcasted_iota(I32, shape, dim)


def dot(a, b):
    return jnp.dot(a, b, preferred_element_type=F32)


def dot_nt(a, b):
    return lax.dot_general(a, b, (((1,), (1,)), ((), ())), preferred_element_type=F32)


def span(ka):
    return max(ka - 1, 0), min(ka + 1, 3)


def rows(start, size):
    return pl.ds(pl.multiple_of(start, size), size)


def split3(x):
    h = x.astype(BF16).astype(F32)
    r = x - h
    m = r.astype(BF16).astype(F32)
    return h, m, r - m


def column(row):
    eye = iota((64, 64), 0) == iota((64, 64), 1)
    return jnp.sum(jnp.where(eye, row, 0.0), axis=1, keepdims=True)


def messages(rec_ref, ql_ref, send_ref):
    home, first, second = rec_ref[0:1], rec_ref[1:2], rec_ref[2:3]
    named = jnp.where(iota((DEVICES, 256), 0) == home, 1.0, 0.0)
    earlier = jnp.where(iota((256, 256), 0) < iota((256, 256), 1), 1.0, 0.0).astype(BF16)
    before = dot(named.astype(BF16), earlier)
    rank = jnp.sum(named * before, axis=0, keepdims=True).astype(I32)
    slot = iota((DEVICES, 256), 0)
    values = jnp.where(slot == rank, first + 1, jnp.where(slot == rank + CAP, second + 1, 0))
    out = dot_nt(named.astype(BF16), values.astype(F32).astype(BF16))
    box = iota((64, 128), 0)
    parent = box // 32 * 4 + box // 8 % 2 * 2 + box % 4 // 2
    charge = jnp.sum(ql_ref[...], axis=1, keepdims=True)
    mine = jnp.where(iota((64, 128), 1) == parent + 2 * CAP, charge, 0.0)
    send_ref[...] = out + jnp.sum(mine, axis=0, keepdims=True)


def planes(pos_ref, wid_ref, left_ref, right_ref):
    box = iota((64, 128), 0)
    cells = (box // 16, box // 4 % 4, box % 4)
    norm = wid_ref[...]
    one, zero = jnp.ones((64, 128), F32), jnp.zeros((64, 128), F32)
    for c in range(3):
        x = pos_ref[c] + (cells[c].astype(F32) - 2.0)
        norm = norm + x * x
        left_ref[c] = -2.0 * x
        right_ref[c] = x
    left_ref[3], right_ref[3] = norm, one
    left_ref[4], right_ref[4] = one, norm
    for c in range(5, 8):
        left_ref[c] = zero
        right_ref[c] = zero


def features(r, left_ref, right_ref, ql_ref, lt_ref, rt_ref, qc_ref):
    eye = jnp.where(iota((128, 128), 0) == iota((128, 128), 1), 1.0, 0.0).astype(BF16)
    pad = jnp.zeros((128 - DEPTH, 128), BF16)
    packed = []
    for k in range(4):
        b = 4 * r + k
        h, m, l = split3(left_ref[:, b, :])
        packed.append(jnp.concatenate([h, h, m, m, h, l], axis=0).astype(BF16))
        h, m, l = split3(right_ref[:, b, :])
        rt_ref[r, :, 128 * k : 128 * k + 128] = jnp.concatenate([h, m, h, m, l, h], axis=0).astype(BF16)
    for k in (0, 2):
        t = dot_nt(eye, jnp.concatenate([packed[k], pad, packed[k + 1], pad], axis=0))
        for kk in (0, 1):
            lt_ref[rows((4 * r + k + kk) * 128, 128), :] = t[:, 128 * kk : 128 * kk + DEPTH].astype(BF16)
    for k in range(4):
        b = 4 * r + k
        h, m, l = split3(jnp.broadcast_to(ql_ref[pl.ds(b, 1), :], (128, 128)))
        t = dot_nt(eye, h.astype(BF16)) + dot_nt(eye, m.astype(BF16)) + dot_nt(eye, l.astype(BF16))
        qc_ref[rows(b * 128, 128), :] = t


def kernel_block(r1, ka, r2, lo, hi, lt_ref, rt_ref):
    left = lt_ref[rows(r1 * 512 + ka * 128, 128), :]
    d = dot(left, rt_ref[r2, :, lo * 128 : (hi + 1) * 128])
    return lax.rsqrt(d) - lax.rsqrt(d + SOFT_TERM)


def produce(r1, r2, slot, lt_ref, rt_ref, k_ref):
    for ka in range(4):
        lo, hi = span(ka)
        k_ref[slot, ka, :, lo * 128 : (hi + 1) * 128] = kernel_block(r1, ka, r2, lo, hi, lt_ref, rt_ref)


def consume(r1, r2, block, spans, ql_ref, qc_ref, cnt_ref, acc1_ref, acc2_ref, diff):
    crow = cnt_ref[pl.ds(r1, 1), :]
    back = {}
    for ka, (lo, hi) in spans:
        k = block(ka)
        qc = qc_ref[rows(r1 * 512 + ka * 128, 128), :].reshape(16, 8, 128)
        total = None
        for kb in range(lo, hi + 1):
            lane = diff * 16 + 4 * ka + kb
            c = jnp.broadcast_to(crow[:, lane : lane + 1], (8, 128))
            kk = k[:, (kb - lo) * 128 : (kb - lo + 1) * 128].reshape(16, 8, 128)
            cq = c * jnp.broadcast_to(ql_ref[pl.ds(4 * r2 + kb, 1), :], (8, 128))
            part = kk * cq[None]
            total = part if total is None else total + part
            b = jnp.sum(kk * qc, axis=0) * c
            back[kb] = b if kb not in back else back[kb] + b
        acc1_ref[4 * r1 + ka] += total.reshape(128, 128)
    for kb, b in back.items():
        acc2_ref[4 * r2 + kb] += b


CROSS = [(ka, span(ka)) for ka in range(4)]
OWN = [(ka, (ka + 1, ka + 1)) for ka in range(3)]


def count_pairs(got, cnt_ref):
    c = jnp.zeros((16, 128), F32)
    for k in range(CAP):
        a, b = got[k : k + 1].astype(I32) - 1, got[CAP + k : CAP + 1 + k].astype(I32) - 1
        first, second = jnp.minimum(a, b), jnp.maximum(a, b)
        r1, r2 = first // 4, second // 4
        lane = (r2 - r1) * 16 + first % 4 * 4 + second % 4
        hot1 = jnp.where(iota((16, 128), 0) == r1, 1.0, 0.0).astype(BF16)
        hot2 = jnp.where((iota((128, 128), 0) == lane) & (first >= 0), 1.0, 0.0).astype(BF16)
        c = c + dot_nt(hot1, hot2)
    cnt_ref[...] = c


def far_field(got, u, v):
    g, src = iota((64, 128), 0), iota((64, 128), 1)
    dx0 = (4 * (u - src % GX) + g // 16).astype(F32) + 0.5
    dy0 = (4 * (v - src // GX) + g // 4 % 4).astype(F32) + 0.5
    dz0 = (g % 4).astype(F32) + 0.5
    total = jnp.zeros((64, 128), F32)
    for p in range(8):
        dx = dx0 - (2 * (p // 4) + 1)
        dy = dy0 - (2 * (p // 2 % 2) + 1)
        dz = dz0 - (2 * (p % 2) + 1)
        total = total + lax.rsqrt(dx * dx + dy * dy + dz * dz + SOFT_TERM) * got[2 * CAP + p : 2 * CAP + 1 + p]
    col = jnp.sum(total, axis=1, keepdims=True)
    eye = iota((64, 64), 0) == iota((64, 64), 1)
    return jnp.sum(jnp.where(eye, col, 0.0), axis=0, keepdims=True)


def collect(acc1_ref, acc2_ref, live, out_ref):
    row = iota((16, 128), 0)

    def step(g, carry):
        total = jnp.zeros((16, 128), F32)
        for k in range(8):
            b = 8 * g + k
            x = acc1_ref[b]
            h = x.astype(BF16)
            low = (x - h.astype(F32)).astype(BF16)
            pick = jnp.where(row == k, 1.0, 0.0).astype(BF16)
            total = total + dot_nt(pick, h) + dot_nt(pick, low)
            s = jnp.sum(acc2_ref[b], axis=0, keepdims=True)
            total = total + jnp.where(row == k, s, 0.0)
        out_ref[rows(8 * g, 8), :] = total[:8]
        return carry

    lax.fori_loop(0, 8, step, 0)
    out_ref[...] = jnp.where(live, out_ref[...], 0.0)


def kernel(
    q_ref, pos_ref, wid_ref, cnt_ref, rec_ref, near_ref, far_ref,
    left_ref, right_ref, lt_ref, rt_ref, ql_ref, qc_ref, k_ref, c_ref, acc1_ref, acc2_ref,
    send_ref, mid_ref, turn_ref, got_ref, send1, recv1, send2, recv2,
):
    u, v = lax.axis_index("gx"), lax.axis_index("gy")
    others_x = [lax.rem(u + s, GX) for s in range(1, GX)]
    others_y = [lax.rem(v + s, GY) for s in range(1, GY)]
    barrier = pltpu.get_barrier_semaphore()
    for x in others_x:
        pl.semaphore_signal(barrier, inc=1, device_id=(x, v), device_id_type=MESH)
    for y in others_y:
        pl.semaphore_signal(barrier, inc=1, device_id=(u, y), device_id_type=MESH)

    cnt = column(cnt_ref[...].astype(F32)).astype(I32)
    live = iota((64, 128), 1) < cnt
    ql_ref[...] = jnp.where(live, q_ref[...], 0.0)
    messages(rec_ref, ql_ref, send_ref)
    pl.semaphore_wait(barrier, GX + GY - 2)

    first = [
        pltpu.make_async_remote_copy(
            src_ref=send_ref.at[rows(x * GY, GY)],
            dst_ref=mid_ref.at[rows(u * GY, GY)],
            send_sem=send1.at[s],
            recv_sem=recv1.at[s],
            device_id=(x, v),
            device_id_type=MESH,
        )
        for s, x in enumerate(others_x)
    ]
    for copy in first:
        copy.start()
    mid_ref[rows(u * GY, GY), :] = send_ref[rows(u * GY, GY), :]

    acc1_ref[...] = jnp.zeros_like(acc1_ref)
    acc2_ref[...] = jnp.zeros_like(acc2_ref)
    planes(pos_ref, wid_ref, left_ref, right_ref)

    def feature_step(r, carry):
        features(r, left_ref, right_ref, ql_ref, lt_ref, rt_ref, qc_ref)
        return carry

    lax.fori_loop(0, 16, feature_step, 0)

    for copy in first:
        copy.wait_recv()
    for y in range(GY):
        turn_ref[y * GX : (y + 1) * GX, :] = mid_ref[pl.ds(y, GX, stride=GY), :]
    second = [
        pltpu.make_async_remote_copy(
            src_ref=turn_ref.at[rows(y * GX, GX)],
            dst_ref=got_ref.at[rows(v * GX, GX)],
            send_sem=send2.at[s],
            recv_sem=recv2.at[s],
            device_id=(u, y),
            device_id_type=MESH,
        )
        for s, y in enumerate(others_y)
    ]
    for copy in second:
        copy.start()
    got_ref[rows(v * GX, GX), :] = turn_ref[rows(v * GX, GX), :]

    def produce_step(i, carry):
        for j in range(3):
            produce(4 * i + j, 4 * i + j + 1, 3 * i + j, lt_ref, rt_ref, k_ref)
        return carry

    lax.fori_loop(0, 4, produce_step, 0)

    for copy in second:
        copy.wait_recv()
    got = got_ref[...].T
    count_pairs(got, c_ref)
    far_ref[...] = far_field(got, u, v)

    sums = (ql_ref, qc_ref, c_ref, acc1_ref, acc2_ref)

    def direct(r1, diff, spans):
        r2, of = r1 + diff, dict(spans)
        consume(r1, r2, lambda ka: kernel_block(r1, ka, r2, *of[ka], lt_ref, rt_ref), spans, *sums, diff)

    for dj in (-1, 1):

        def diagonal_step(i, carry, dj=dj):
            for j in range(3):
                direct(4 * i + j + (dj < 0), 4 + dj, CROSS)
            return carry

        lax.fori_loop(0, 3, diagonal_step, 0)

    def straight_step(i, carry):
        for j in range(4):
            p = 4 * i + j
            direct(p, 4, CROSS)

            def block(ka, p=p):
                lo, hi = span(ka)
                return k_ref[p, ka, :, lo * 128 : (hi + 1) * 128]

            r1 = p // 3 * 4 + p % 3
            consume(r1, r1 + 1, block, CROSS, *sums, 1)
        return carry

    lax.fori_loop(0, 3, straight_step, 0)

    def own_step(i, carry):
        for j in range(4):
            direct(4 * i + j, 0, OWN)
        return carry

    lax.fori_loop(0, 4, own_step, 0)

    collect(acc1_ref, acc2_ref, live, near_ref)
    for copy in first + second:
        copy.wait_send()


def body(charges, positions, widths, site_counts, pair_records):
    vmem = pltpu.VMEM
    near, far = pl.pallas_call(
        kernel,
        out_shape=(jax.ShapeDtypeStruct((64, 128), F32), jax.ShapeDtypeStruct((1, 64), F32)),
        in_specs=[pl.BlockSpec(memory_space=vmem)] * 5,
        out_specs=(pl.BlockSpec(memory_space=vmem),) * 2,
        scratch_shapes=[
            vmem((8, 64, 128), F32),
            vmem((8, 64, 128), F32),
            vmem((8192, DEPTH), BF16),
            vmem((16, DEPTH, 512), BF16),
            vmem((64, 128), F32),
            vmem((8192, 128), F32),
            vmem((12, 4, 128, 512), F32),
            vmem((16, 128), F32),
            vmem((64, 128, 128), F32),
            vmem((64, 8, 128), F32),
            vmem((DEVICES, 128), F32),
            vmem((DEVICES, 128), F32),
            vmem((DEVICES, 128), F32),
            vmem((DEVICES, 128), F32),
            pltpu.SemaphoreType.DMA((GX - 1,)),
            pltpu.SemaphoreType.DMA((GX - 1,)),
            pltpu.SemaphoreType.DMA((GY - 1,)),
            pltpu.SemaphoreType.DMA((GY - 1,)),
        ],
        compiler_params=pltpu.CompilerParams(collective_id=0, has_side_effects=True, vmem_limit_bytes=56 << 20),
    )(charges, positions.transpose(1, 0, 2), widths, site_counts.reshape(1, 64), pair_records.T)
    return near, far.reshape(64)


def solution(mesh):
    return jax.shard_map(
        body,
        mesh=mesh,
        in_specs=(
            P(("gx", "gy"), None),
            P(("gx", "gy"), None, None),
            P(("gx", "gy"), None),
            P(("gx", "gy")),
            P(("gx", "gy"), None),
        ),
        out_specs=(P(("gx", "gy"), None), P(("gx", "gy"))),
        check_vma=False,
    )
```

```python
import jax
import jax.numpy as jnp
from jax import lax
from jax.experimental import pallas as pl
from jax.experimental.pallas import tpu as pltpu
from jax.sharding import PartitionSpec as P

F32, BF16, I32 = jnp.float32, jnp.bfloat16, jnp.int32
MESH = pl.DeviceIdType.MESH
GX, GY, CAP = 8, 16, 8
DEVICES = GX * GY
DEPTH = 48
SOFT_TERM = 2.0


def iota(shape, dim):
    return lax.broadcasted_iota(I32, shape, dim)


def dot(a, b):
    return jnp.dot(a, b, preferred_element_type=F32)


def dot_nt(a, b):
    return lax.dot_general(a, b, (((1,), (1,)), ((), ())), preferred_element_type=F32)


def span(ka):
    return max(ka - 1, 0), min(ka + 1, 3)


def rows(start, size):
    return pl.ds(pl.multiple_of(start, size), size)


def split3(x):
    h = x.astype(BF16).astype(F32)
    r = x - h
    m = r.astype(BF16).astype(F32)
    return h, m, r - m


def column(row):
    eye = iota((64, 64), 0) == iota((64, 64), 1)
    return jnp.sum(jnp.where(eye, row, 0.0), axis=1, keepdims=True)


def messages(rec_ref, ql_ref, send_ref):
    home, first, second = rec_ref[0:1], rec_ref[1:2], rec_ref[2:3]
    named = jnp.where(iota((DEVICES, 256), 0) == home, 1.0, 0.0)
    earlier = jnp.where(iota((256, 256), 0) < iota((256, 256), 1), 1.0, 0.0).astype(BF16)
    before = dot(named.astype(BF16), earlier)
    rank = jnp.sum(named * before, axis=0, keepdims=True).astype(I32)
    slot = iota((DEVICES, 256), 0)
    values = jnp.where(slot == rank, first + 1, jnp.where(slot == rank + CAP, second + 1, 0))
    out = dot_nt(named.astype(BF16), values.astype(F32).astype(BF16))
    box = iota((64, 128), 0)
    parent = box // 32 * 4 + box // 8 % 2 * 2 + box % 4 // 2
    charge = jnp.sum(ql_ref[...], axis=1, keepdims=True)
    mine = jnp.where(iota((64, 128), 1) == parent + 2 * CAP, charge, 0.0)
    send_ref[...] = out + jnp.sum(mine, axis=0, keepdims=True)


def planes(pos_ref, wid_ref, left_ref, right_ref):
    box = iota((64, 128), 0)
    cells = (box // 16, box // 4 % 4, box % 4)
    norm = wid_ref[...]
    one = jnp.ones((64, 128), F32)
    for c in range(3):
        x = pos_ref[c] + (cells[c].astype(F32) - 2.0)
        norm = norm + x * x
        left_ref[64 * c : 64 * c + 64] = -2.0 * x
        right_ref[64 * c : 64 * c + 64] = x
    left_ref[192:256], right_ref[192:256] = norm, one
    left_ref[256:320], right_ref[256:320] = one, norm
    left_ref[320:512] = jnp.zeros((192, 128), F32)
    right_ref[320:512] = jnp.zeros((192, 128), F32)


def features(g, left_ref, right_ref, ql_ref, lt_ref, rt_ref, qc_ref):
    eye = jnp.where(iota((128, 128), 0) == iota((128, 128), 1), 1.0, 0.0).astype(BF16)
    pad = jnp.zeros((128 - DEPTH, 128), BF16)
    packed = []
    for k in range(8):
        b = 8 * g + k
        h, m, l = split3(left_ref[pl.ds(b, 8, stride=64), :])
        packed.append(jnp.concatenate([h, h, m, m, h, l], axis=0).astype(BF16))
        h, m, l = split3(right_ref[pl.ds(b, 8, stride=64), :])
        lanes = slice(128 * (k % 4), 128 * (k % 4) + 128)
        rt_ref[2 * g + k // 4, :, lanes] = jnp.concatenate([h, m, h, m, l, h], axis=0).astype(BF16)
    for k in range(0, 8, 2):
        t = dot_nt(eye, jnp.concatenate([packed[k], pad, packed[k + 1], pad], axis=0))
        for kk in (0, 1):
            lt_ref[rows((8 * g + k + kk) * 128, 128), :] = t[:, 128 * kk : 128 * kk + DEPTH].astype(BF16)
    q = ql_ref[rows(8 * g, 8), :].T
    for k in range(8):
        qc_ref[rows((8 * g + k) * 128, 128), :] = jnp.broadcast_to(q[:, k : k + 1], (128, 128))


CROSS = [(ka, kb) for ka in range(4) for kb in range(span(ka)[0], span(ka)[1] + 1)]
OWN = [(ka, ka + 1) for ka in range(3)]
PAIRS = 42


def produce(r1, r2, spans, index, lt_ref, rt_ref, qc_ref, k_ref, back_ref):
    for ka, lo, hi in spans:
        left = lt_ref[rows(r1 * 512 + ka * 128, 128), :]
        d = dot(left, rt_ref[r2, :, lo * 128 : (hi + 1) * 128])
        kern = lax.rsqrt(d) - lax.rsqrt(d + SOFT_TERM)
        qc = qc_ref[rows(r1 * 512 + ka * 128, 128), :].reshape(16, 8, 128)
        for kb in range(lo, hi + 1):
            kk = kern[:, (kb - lo) * 128 : (kb - lo + 1) * 128]
            k_ref[index(ka, kb)] = kk
            back_ref[index(ka, kb)] = jnp.sum(kk.reshape(16, 8, 128) * qc, axis=0)


CROSS_SPANS = [(ka, *span(ka)) for ka in range(4)]
OWN_SPANS = [(ka, ka + 1, ka + 1) for ka in range(3)]


def cross_index(slot):
    return lambda ka, kb: slot * len(CROSS) + CROSS.index((ka, kb))


def own_index(row):
    return lambda ka, kb: PAIRS * len(CROSS) + row * len(OWN) + ka


def produce_three(t, *refs):
    g4, g7, g10 = (t + 10) // 14, t // 7, t // 10
    i = t - 4 * g4 - 3 * g7 - 3 * g10
    base = 4 * i + g4 - g7 - i * g10
    diff = 1 + 2 * g4 + 2 * g7 - g10
    for j in range(3):
        produce(base + j, base + j + diff, CROSS_SPANS, cross_index(3 * t + j), *refs)


def produce_own(t, *refs):
    for j in range(4):
        r = 4 * t + j
        produce(r, r, OWN_SPANS, own_index(r), *refs)


def consume(r1, parts, ql_ref, cnt_ref, k_ref, back_ref, col_ref, acc_ref):
    crow = jnp.broadcast_to(cnt_ref[pl.ds(r1, 1), :], (8, 128))
    lanes = iota((128, 128), 1)
    totals = [None] * 4
    for diff, pairs, index in parts:
        back = {}
        for ka, kb in pairs:
            lane = diff * 16 + 4 * ka + kb
            c = jnp.broadcast_to(crow[:, lane : lane + 1], (8, 128))
            cq = c * jnp.broadcast_to(ql_ref[pl.ds(4 * (r1 + diff) + kb, 1), :], (8, 128))
            part = k_ref[index(ka, kb)].reshape(16, 8, 128) * cq[None]
            totals[ka] = part if totals[ka] is None else totals[ka] + part
            b = back_ref[index(ka, kb)] * c
            back[kb] = b if kb not in back else back[kb] + b
        for kb, b in back.items():
            acc_ref[rows((4 * (r1 + diff) + kb) * 8, 8), :] += b
    for ka in range(4):
        if totals[ka] is not None:
            total = jnp.sum(totals[ka].reshape(128, 128), axis=1, keepdims=True)
            col_ref[...] = jnp.where(lanes == 4 * r1 + ka, total, col_ref[...])


def consume_all(*refs):
    def step(i, carry):
        for j in range(4):
            r1 = 4 * i + j
            parts = [(0, OWN, own_index(r1)), (4, CROSS, cross_index(30 + r1))]
            if j <= 2:
                parts.append((1, CROSS, cross_index(3 * i + j)))
                parts.append((5, CROSS, cross_index(21 + 3 * i + j)))
            if j >= 1:
                parts.append((3, CROSS, cross_index(12 + 3 * i + j - 1)))
            consume(r1, parts, *refs)
        return carry

    lax.fori_loop(0, 3, step, 0)
    for j in range(4):
        parts = [(0, OWN, own_index(12 + j))]
        if j <= 2:
            parts.append((1, CROSS, cross_index(9 + j)))
        consume(12 + j, parts, *refs)


def count_pairs(got, cnt_ref):
    c = jnp.zeros((16, 128), F32)
    for k in range(CAP):
        a, b = got[k : k + 1].astype(I32) - 1, got[CAP + k : CAP + 1 + k].astype(I32) - 1
        first, second = jnp.minimum(a, b), jnp.maximum(a, b)
        r1, r2 = first // 4, second // 4
        lane = (r2 - r1) * 16 + first % 4 * 4 + second % 4
        hot1 = jnp.where(iota((16, 128), 0) == r1, 1.0, 0.0).astype(BF16)
        hot2 = jnp.where((iota((128, 128), 0) == lane) & (first >= 0), 1.0, 0.0).astype(BF16)
        c = c + dot_nt(hot1, hot2)
    cnt_ref[...] = c


def far_field(got, u, v):
    g, src = iota((64, 128), 0), iota((64, 128), 1)
    dx0 = (4 * (u - src % GX) + g // 16).astype(F32) + 0.5
    dy0 = (4 * (v - src // GX) + g // 4 % 4).astype(F32) + 0.5
    dz0 = (g % 4).astype(F32) + 0.5
    total = jnp.zeros((64, 128), F32)
    for p in range(8):
        dx = dx0 - (2 * (p // 4) + 1)
        dy = dy0 - (2 * (p // 2 % 2) + 1)
        dz = dz0 - (2 * (p % 2) + 1)
        total = total + lax.rsqrt(dx * dx + dy * dy + dz * dz + SOFT_TERM) * got[2 * CAP + p : 2 * CAP + 1 + p]
    col = jnp.sum(total, axis=1, keepdims=True)
    eye = iota((64, 64), 0) == iota((64, 64), 1)
    return jnp.sum(jnp.where(eye, col, 0.0), axis=0, keepdims=True)


def collect(col_ref, acc_ref, live, out_ref):
    total = col_ref[...].T[:64]
    for sub in range(8):
        part = [acc_ref[pl.ds(64 * g + sub, 8, stride=8), :] for g in range(8)]
        total = total + jnp.concatenate(part, axis=0)
    out_ref[...] = jnp.where(live, total, 0.0)


def kernel(
    q_ref, pos_ref, wid_ref, cnt_ref, rec_ref, near_ref, far_ref,
    left_ref, right_ref, lt_ref, rt_ref, ql_ref, qc_ref, k_ref, back_ref, c_ref, col_ref, acc_ref,
    send_ref, mid_ref, turn_ref, got_ref, send1, recv1, send2, recv2,
):
    u, v = lax.axis_index("gx"), lax.axis_index("gy")
    others_x = [lax.rem(u + s, GX) for s in range(1, GX)]
    others_y = [lax.rem(v + s, GY) for s in range(1, GY)]
    barrier = pltpu.get_barrier_semaphore()
    for x in others_x:
        pl.semaphore_signal(barrier, inc=1, device_id=(x, v), device_id_type=MESH)
    for y in others_y:
        pl.semaphore_signal(barrier, inc=1, device_id=(u, y), device_id_type=MESH)

    cnt = column(cnt_ref[...].astype(F32)).astype(I32)
    live = iota((64, 128), 1) < cnt
    ql_ref[...] = jnp.where(live, q_ref[...], 0.0)
    messages(rec_ref, ql_ref, send_ref)

    later = 4 * (v % 4) + 5 * (v // 4) + 8 * (u // 2)
    early = jnp.maximum(0, 52 - later)
    features_first = jnp.minimum(4, early // 5)
    pairs_first = jnp.maximum(0, early - 12) // 7
    pairs_second = pairs_first + 1 + jnp.minimum(early, 12) // 12

    def feature_step(t, carry):
        for g in range(2):
            features(2 * t + g, left_ref, right_ref, ql_ref, lt_ref, rt_ref, qc_ref)
        return carry

    def produce_step(t, carry):
        produce_three(t, lt_ref, rt_ref, qc_ref, k_ref, back_ref)
        return carry

    def own_step(t, carry):
        produce_own(t, lt_ref, rt_ref, qc_ref, k_ref, back_ref)
        return carry

    planes(pos_ref, wid_ref, left_ref, right_ref)
    lax.fori_loop(0, features_first, feature_step, 0)
    lax.fori_loop(0, pairs_first, produce_step, 0)

    pl.semaphore_wait(barrier, GX + GY - 2)
    first = [
        pltpu.make_async_remote_copy(
            src_ref=send_ref.at[rows(x * GY, GY)],
            dst_ref=mid_ref.at[rows(u * GY, GY)],
            send_sem=send1.at[s],
            recv_sem=recv1.at[s],
            device_id=(x, v),
            device_id_type=MESH,
        )
        for s, x in enumerate(others_x)
    ]
    for copy in first:
        copy.start()
    mid_ref[rows(u * GY, GY), :] = send_ref[rows(u * GY, GY), :]

    lax.fori_loop(features_first, 4, feature_step, 0)
    lax.fori_loop(pairs_first, pairs_second, produce_step, 0)

    for copy in first:
        copy.wait_recv()
    for y in range(GY):
        turn_ref[y * GX : (y + 1) * GX, :] = mid_ref[pl.ds(y, GX, stride=GY), :]
    second = [
        pltpu.make_async_remote_copy(
            src_ref=turn_ref.at[rows(y * GX, GX)],
            dst_ref=got_ref.at[rows(v * GX, GX)],
            send_sem=send2.at[s],
            recv_sem=recv2.at[s],
            device_id=(u, y),
            device_id_type=MESH,
        )
        for s, y in enumerate(others_y)
    ]
    for copy in second:
        copy.start()
    got_ref[rows(v * GX, GX), :] = turn_ref[rows(v * GX, GX), :]

    lax.fori_loop(pairs_second, PAIRS // 3, produce_step, 0)
    lax.fori_loop(0, 4, own_step, 0)
    acc_ref[...] = jnp.zeros_like(acc_ref)
    col_ref[...] = jnp.zeros_like(col_ref)

    for copy in second:
        copy.wait_recv()
    got = got_ref[...].T
    count_pairs(got, c_ref)
    far_ref[...] = far_field(got, u, v)
    consume_all(ql_ref, c_ref, k_ref, back_ref, col_ref, acc_ref)
    collect(col_ref, acc_ref, live, near_ref)
    for copy in first + second:
        copy.wait_send()


def body(charges, positions, widths, site_counts, pair_records):
    vmem = pltpu.VMEM
    near, far = pl.pallas_call(
        kernel,
        out_shape=(jax.ShapeDtypeStruct((64, 128), F32), jax.ShapeDtypeStruct((1, 64), F32)),
        in_specs=[pl.BlockSpec(memory_space=vmem)] * 5,
        out_specs=(pl.BlockSpec(memory_space=vmem),) * 2,
        scratch_shapes=[
            vmem((512, 128), F32),
            vmem((512, 128), F32),
            vmem((8192, DEPTH), BF16),
            vmem((16, DEPTH, 512), BF16),
            vmem((64, 128), F32),
            vmem((8192, 128), F32),
            vmem((468, 128, 128), F32),
            vmem((468, 8, 128), F32),
            vmem((16, 128), F32),
            vmem((128, 128), F32),
            vmem((512, 128), F32),
            vmem((DEVICES, 128), F32),
            vmem((DEVICES, 128), F32),
            vmem((DEVICES, 128), F32),
            vmem((DEVICES, 128), F32),
            pltpu.SemaphoreType.DMA((GX - 1,)),
            pltpu.SemaphoreType.DMA((GX - 1,)),
            pltpu.SemaphoreType.DMA((GY - 1,)),
            pltpu.SemaphoreType.DMA((GY - 1,)),
        ],
        compiler_params=pltpu.CompilerParams(collective_id=0, has_side_effects=True, vmem_limit_bytes=56 << 20),
    )(charges, positions.transpose(1, 0, 2), widths, site_counts.reshape(1, 64), pair_records.T)
    return near, far.reshape(64)


def solution(mesh):
    return jax.shard_map(
        body,
        mesh=mesh,
        in_specs=(
            P(("gx", "gy"), None),
            P(("gx", "gy"), None, None),
            P(("gx", "gy"), None),
            P(("gx", "gy")),
            P(("gx", "gy"), None),
        ),
        out_specs=(P(("gx", "gy"), None), P(("gx", "gy"))),
        check_vma=False,
    )
```

```python
import jax
import jax.numpy as jnp
from jax import lax
from jax.experimental import pallas as pl
from jax.experimental.pallas import tpu as pltpu
from jax.sharding import PartitionSpec as P

F32, BF16, I32 = jnp.float32, jnp.bfloat16, jnp.int32
MESH = pl.DeviceIdType.MESH
GX, GY, CAP = 8, 16, 8
DEVICES = GX * GY
DEPTH = 48
SOFT_TERM = 2.0


def iota(shape, dim):
    return lax.broadcasted_iota(I32, shape, dim)


def dot(a, b):
    return jnp.dot(a, b, preferred_element_type=F32)


def dot_nt(a, b):
    return lax.dot_general(a, b, (((1,), (1,)), ((), ())), preferred_element_type=F32)


def span(ka):
    return max(ka - 1, 0), min(ka + 1, 3)


def rows(start, size):
    return pl.ds(pl.multiple_of(start, size), size)


def split3(x):
    h = x.astype(BF16).astype(F32)
    r = x - h
    m = r.astype(BF16).astype(F32)
    return h, m, r - m


def column(row):
    eye = iota((64, 64), 0) == iota((64, 64), 1)
    return jnp.sum(jnp.where(eye, row, 0.0), axis=1, keepdims=True)


def messages(rec_ref, ql_ref, send_ref):
    home, first, second = rec_ref[0:1], rec_ref[1:2], rec_ref[2:3]
    named = jnp.where(iota((DEVICES, 256), 0) == home, 1.0, 0.0)
    earlier = jnp.where(iota((256, 256), 0) < iota((256, 256), 1), 1.0, 0.0).astype(BF16)
    before = dot(named.astype(BF16), earlier)
    rank = jnp.sum(named * before, axis=0, keepdims=True).astype(I32)
    slot = iota((DEVICES, 256), 0)
    values = jnp.where(slot == rank, first + 1, jnp.where(slot == rank + CAP, second + 1, 0))
    out = dot_nt(named.astype(BF16), values.astype(F32).astype(BF16))
    box = iota((64, 128), 0)
    parent = box // 32 * 4 + box // 8 % 2 * 2 + box % 4 // 2
    charge = jnp.sum(ql_ref[...], axis=1, keepdims=True)
    mine = jnp.where(iota((64, 128), 1) == parent + 2 * CAP, charge, 0.0)
    send_ref[...] = out + jnp.sum(mine, axis=0, keepdims=True)


def planes(pos_ref, wid_ref, left_ref, right_ref):
    box = iota((64, 128), 0)
    cells = (box // 16, box // 4 % 4, box % 4)
    norm = wid_ref[...]
    one = jnp.ones((64, 128), F32)
    for c in range(3):
        x = pos_ref[c] + (cells[c].astype(F32) - 2.0)
        norm = norm + x * x
        left_ref[64 * c : 64 * c + 64] = -2.0 * x
        right_ref[64 * c : 64 * c + 64] = x
    left_ref[192:256], right_ref[192:256] = norm, one
    left_ref[256:320], right_ref[256:320] = one, norm
    left_ref[320:512] = jnp.zeros((192, 128), F32)
    right_ref[320:512] = jnp.zeros((192, 128), F32)


def features(g, left_ref, right_ref, ql_ref, lt_ref, rt_ref, qc_ref):
    eye = jnp.where(iota((128, 128), 0) == iota((128, 128), 1), 1.0, 0.0).astype(BF16)
    pad = jnp.zeros((128 - DEPTH, 128), BF16)
    packed = []
    for k in range(8):
        b = 8 * g + k
        h, m, l = split3(left_ref[pl.ds(b, 8, stride=64), :])
        packed.append(jnp.concatenate([h, h, m, m, h, l], axis=0).astype(BF16))
        h, m, l = split3(right_ref[pl.ds(b, 8, stride=64), :])
        lanes = slice(128 * (k % 4), 128 * (k % 4) + 128)
        rt_ref[2 * g + k // 4, :, lanes] = jnp.concatenate([h, m, h, m, l, h], axis=0).astype(BF16)
    for k in range(0, 8, 2):
        t = dot_nt(eye, jnp.concatenate([packed[k], pad, packed[k + 1], pad], axis=0))
        for kk in (0, 1):
            lt_ref[rows((8 * g + k + kk) * 128, 128), :] = t[:, 128 * kk : 128 * kk + DEPTH].astype(BF16)
    q = ql_ref[rows(8 * g, 8), :].T
    for k in range(8):
        qc_ref[rows((8 * g + k) * 128, 128), :] = jnp.broadcast_to(q[:, k : k + 1], (128, 128))


CROSS = [(ka, kb) for ka in range(4) for kb in range(span(ka)[0], span(ka)[1] + 1)]
OWN = [(ka, ka + 1) for ka in range(3)]
PAIRS = 42


def produce(r1, r2, spans, index, lt_ref, rt_ref, qc_ref, k_ref, back_ref):
    for ka, lo, hi in spans:
        left = lt_ref[rows(r1 * 512 + ka * 128, 128), :]
        d = dot(left, rt_ref[r2, :, lo * 128 : (hi + 1) * 128])
        kern = lax.rsqrt(d) - lax.rsqrt(d + SOFT_TERM)
        qc = qc_ref[rows(r1 * 512 + ka * 128, 128), :].reshape(16, 8, 128)
        for kb in range(lo, hi + 1):
            kk = kern[:, (kb - lo) * 128 : (kb - lo + 1) * 128]
            k_ref[index(ka, kb)] = kk
            back_ref[index(ka, kb)] = jnp.sum(kk.reshape(16, 8, 128) * qc, axis=0)


CROSS_SPANS = [(ka, *span(ka)) for ka in range(4)]
OWN_SPANS = [(ka, ka + 1, ka + 1) for ka in range(3)]


def cross_index(slot):
    return lambda ka, kb: slot * len(CROSS) + CROSS.index((ka, kb))


def own_index(row):
    return lambda ka, kb: PAIRS * len(CROSS) + row * len(OWN) + ka


def produce_three(t, *refs):
    g4, g7, g10 = (t + 10) // 14, t // 7, t // 10
    i = t - 4 * g4 - 3 * g7 - 3 * g10
    base = 4 * i + g4 - g7 - i * g10
    diff = 1 + 2 * g4 + 2 * g7 - g10
    for j in range(3):
        produce(base + j, base + j + diff, CROSS_SPANS, cross_index(3 * t + j), *refs)


def produce_own(t, *refs):
    for j in range(4):
        r = 4 * t + j
        produce(r, r, OWN_SPANS, own_index(r), *refs)


def consume(r1, parts, ql_ref, cnt_ref, k_ref, back_ref, col_ref, acc_ref):
    crow = jnp.broadcast_to(cnt_ref[pl.ds(r1, 1), :], (8, 128))
    lanes = iota((128, 128), 1)
    totals = [None] * 4
    for diff, pairs, index in parts:
        back = {}
        for ka, kb in pairs:
            lane = diff * 16 + 4 * ka + kb
            c = jnp.broadcast_to(crow[:, lane : lane + 1], (8, 128))
            cq = c * jnp.broadcast_to(ql_ref[pl.ds(4 * (r1 + diff) + kb, 1), :], (8, 128))
            part = k_ref[index(ka, kb)].reshape(16, 8, 128) * cq[None]
            totals[ka] = part if totals[ka] is None else totals[ka] + part
            b = back_ref[index(ka, kb)] * c
            back[kb] = b if kb not in back else back[kb] + b
        for kb, b in back.items():
            acc_ref[rows((4 * (r1 + diff) + kb) * 8, 8), :] += b
    for ka in range(4):
        if totals[ka] is not None:
            total = jnp.sum(totals[ka].reshape(128, 128), axis=1, keepdims=True)
            col_ref[...] = jnp.where(lanes == 4 * r1 + ka, total, col_ref[...])


def consume_all(*refs):
    def step(i, carry):
        for j in range(4):
            r1 = 4 * i + j
            parts = [(0, OWN, own_index(r1)), (4, CROSS, cross_index(30 + r1))]
            if j <= 2:
                parts.append((1, CROSS, cross_index(3 * i + j)))
                parts.append((5, CROSS, cross_index(21 + 3 * i + j)))
            if j >= 1:
                parts.append((3, CROSS, cross_index(12 + 3 * i + j - 1)))
            consume(r1, parts, *refs)
        return carry

    lax.fori_loop(0, 3, step, 0)
    for j in range(4):
        parts = [(0, OWN, own_index(12 + j))]
        if j <= 2:
            parts.append((1, CROSS, cross_index(9 + j)))
        consume(12 + j, parts, *refs)


def count_pairs(got, cnt_ref):
    c = jnp.zeros((16, 128), F32)
    for k in range(CAP):
        a, b = got[k : k + 1].astype(I32) - 1, got[CAP + k : CAP + 1 + k].astype(I32) - 1
        first, second = jnp.minimum(a, b), jnp.maximum(a, b)
        r1, r2 = first // 4, second // 4
        lane = (r2 - r1) * 16 + first % 4 * 4 + second % 4
        hot1 = jnp.where(iota((16, 128), 0) == r1, 1.0, 0.0).astype(BF16)
        hot2 = jnp.where((iota((128, 128), 0) == lane) & (first >= 0), 1.0, 0.0).astype(BF16)
        c = c + dot_nt(hot1, hot2)
    cnt_ref[...] = c


def far_field(got, u, v):
    g, src = iota((64, 128), 0), iota((64, 128), 1)
    dx0 = (4 * (u - src % GX) + g // 16).astype(F32) + 0.5
    dy0 = (4 * (v - src // GX) + g // 4 % 4).astype(F32) + 0.5
    dz0 = (g % 4).astype(F32) + 0.5
    total = jnp.zeros((64, 128), F32)
    for p in range(8):
        dx = dx0 - (2 * (p // 4) + 1)
        dy = dy0 - (2 * (p // 2 % 2) + 1)
        dz = dz0 - (2 * (p % 2) + 1)
        total = total + lax.rsqrt(dx * dx + dy * dy + dz * dz + SOFT_TERM) * got[2 * CAP + p : 2 * CAP + 1 + p]
    col = jnp.sum(total, axis=1, keepdims=True)
    eye = iota((64, 64), 0) == iota((64, 64), 1)
    return jnp.sum(jnp.where(eye, col, 0.0), axis=0, keepdims=True)


def collect(col_ref, acc_ref, live, out_ref):
    total = col_ref[...].T[:64]
    for sub in range(8):
        part = [acc_ref[pl.ds(64 * g + sub, 8, stride=8), :] for g in range(8)]
        total = total + jnp.concatenate(part, axis=0)
    out_ref[...] = jnp.where(live, total, 0.0)


def kernel(
    q_hbm, pos_hbm, wid_hbm, cnt_hbm, rec_hbm, near_ref, far_ref, q_ref, pos_ref, wid_ref, cnt_ref, rec_ref, in_sem,
    left_ref, right_ref, lt_ref, rt_ref, ql_ref, qc_ref, k_ref, back_ref, c_ref, col_ref, acc_ref,
    send_ref, mid_ref, turn_ref, got_ref, send1, recv1, send2, recv2,
):
    u, v = lax.axis_index("gx"), lax.axis_index("gy")
    pairs = ((rec_hbm, rec_ref), (cnt_hbm, cnt_ref), (q_hbm, q_ref), (pos_hbm, pos_ref), (wid_hbm, wid_ref))
    inputs = [pltpu.make_async_copy(a, b, in_sem.at[s]) for s, (a, b) in enumerate(pairs)]
    for copy in inputs:
        copy.start()
    others_x = [lax.rem(u + s, GX) for s in range(1, GX)]
    others_y = [lax.rem(v + s, GY) for s in range(1, GY)]
    barrier = pltpu.get_barrier_semaphore()
    for x in others_x:
        pl.semaphore_signal(barrier, inc=1, device_id=(x, v), device_id_type=MESH)
    for y in others_y:
        pl.semaphore_signal(barrier, inc=1, device_id=(u, y), device_id_type=MESH)

    for copy in inputs[:3]:
        copy.wait()
    cnt = column(cnt_ref[...].astype(F32)).astype(I32)
    live = iota((64, 128), 1) < cnt
    ql_ref[...] = jnp.where(live, q_ref[...], 0.0)
    messages(rec_ref, ql_ref, send_ref)

    wave = 40 * (v % 4) + 48 * (v // 4)
    enter = 100 + wave + 82 * (u // 2)
    all_in = 100 + jnp.maximum(246 + wave, 264 + 82 * (u // 2)) + 150
    crossed = 1110
    ready = enter + 80
    features_first = jnp.clip((all_in - ready) // 50, 0, 4)
    pairs_first = jnp.clip((all_in - ready - 200) // 65, 0, 14)
    pairs_second = jnp.clip((crossed - ready - 200) // 65, pairs_first, 14)

    def feature_step(t, carry):
        for g in range(2):
            features(2 * t + g, left_ref, right_ref, ql_ref, lt_ref, rt_ref, qc_ref)
        return carry

    def produce_step(t, carry):
        produce_three(t, lt_ref, rt_ref, qc_ref, k_ref, back_ref)
        return carry

    def own_step(t, carry):
        produce_own(t, lt_ref, rt_ref, qc_ref, k_ref, back_ref)
        return carry

    for copy in inputs[3:]:
        copy.wait()
    planes(pos_ref, wid_ref, left_ref, right_ref)
    lax.fori_loop(0, features_first, feature_step, 0)
    lax.fori_loop(0, pairs_first, produce_step, 0)

    pl.semaphore_wait(barrier, GX + GY - 2)
    first = [
        pltpu.make_async_remote_copy(
            src_ref=send_ref.at[rows(x * GY, GY)],
            dst_ref=mid_ref.at[rows(u * GY, GY)],
            send_sem=send1.at[s],
            recv_sem=recv1.at[s],
            device_id=(x, v),
            device_id_type=MESH,
        )
        for s, x in enumerate(others_x)
    ]
    for copy in first:
        copy.start()
    mid_ref[rows(u * GY, GY), :] = send_ref[rows(u * GY, GY), :]

    lax.fori_loop(features_first, 4, feature_step, 0)
    lax.fori_loop(pairs_first, pairs_second, produce_step, 0)

    for copy in first:
        copy.wait_recv()
    for y in range(GY):
        turn_ref[y * GX : (y + 1) * GX, :] = mid_ref[pl.ds(y, GX, stride=GY), :]
    second = [
        pltpu.make_async_remote_copy(
            src_ref=turn_ref.at[rows(y * GX, GX)],
            dst_ref=got_ref.at[rows(v * GX, GX)],
            send_sem=send2.at[s],
            recv_sem=recv2.at[s],
            device_id=(u, y),
            device_id_type=MESH,
        )
        for s, y in enumerate(others_y)
    ]
    for copy in second:
        copy.start()
    got_ref[rows(v * GX, GX), :] = turn_ref[rows(v * GX, GX), :]

    lax.fori_loop(pairs_second, PAIRS // 3, produce_step, 0)
    lax.fori_loop(0, 4, own_step, 0)
    acc_ref[...] = jnp.zeros_like(acc_ref)
    col_ref[...] = jnp.zeros_like(col_ref)

    for copy in second:
        copy.wait_recv()
    got = got_ref[...].T
    count_pairs(got, c_ref)
    far_ref[...] = far_field(got, u, v)
    consume_all(ql_ref, c_ref, k_ref, back_ref, col_ref, acc_ref)
    collect(col_ref, acc_ref, live, near_ref)
    for copy in first + second:
        copy.wait_send()


def body(charges, positions, widths, site_counts, pair_records):
    vmem = pltpu.VMEM
    near, far = pl.pallas_call(
        kernel,
        out_shape=(vmem((64, 128), F32), vmem((1, 64), F32)),
        in_specs=[pl.BlockSpec(memory_space=pl.ANY)] * 5,
        out_specs=(pl.BlockSpec(memory_space=vmem),) * 2,
        scratch_shapes=[
            vmem((64, 128), F32),
            vmem((3, 64, 128), F32),
            vmem((64, 128), F32),
            vmem((1, 64), I32),
            vmem((3, 256), I32),
            pltpu.SemaphoreType.DMA((5,)),
            vmem((512, 128), F32),
            vmem((512, 128), F32),
            vmem((8192, DEPTH), BF16),
            vmem((16, DEPTH, 512), BF16),
            vmem((64, 128), F32),
            vmem((8192, 128), F32),
            vmem((468, 128, 128), F32),
            vmem((468, 8, 128), F32),
            vmem((16, 128), F32),
            vmem((128, 128), F32),
            vmem((512, 128), F32),
            vmem((DEVICES, 128), F32),
            vmem((DEVICES, 128), F32),
            vmem((DEVICES, 128), F32),
            vmem((DEVICES, 128), F32),
            pltpu.SemaphoreType.DMA((GX - 1,)),
            pltpu.SemaphoreType.DMA((GX - 1,)),
            pltpu.SemaphoreType.DMA((GY - 1,)),
            pltpu.SemaphoreType.DMA((GY - 1,)),
        ],
        compiler_params=pltpu.CompilerParams(collective_id=0, has_side_effects=True, vmem_limit_bytes=56 << 20),
    )(charges, positions.transpose(1, 0, 2), widths, site_counts.reshape(1, 64), pair_records.T)
    return near, far.reshape(64)


def solution(mesh):
    return jax.shard_map(
        body,
        mesh=mesh,
        in_specs=(
            P(("gx", "gy"), None),
            P(("gx", "gy"), None, None),
            P(("gx", "gy"), None),
            P(("gx", "gy")),
            P(("gx", "gy"), None),
        ),
        out_specs=(P(("gx", "gy"), None), P(("gx", "gy"))),
        check_vma=False,
    )
```

```python
import jax
import jax.numpy as jnp
from jax import lax
from jax.experimental import pallas as pl
from jax.experimental.pallas import tpu as pltpu
from jax.sharding import PartitionSpec as P

F32, BF16, I32 = jnp.float32, jnp.bfloat16, jnp.int32
MESH = pl.DeviceIdType.MESH
GX, GY, CAP = 8, 16, 8
DEVICES = GX * GY
DEPTH = 48
SOFT_TERM = 2.0
FEATURE_TIME, STEP_TIME = 150, 136


def iota(shape, dim):
    return lax.broadcasted_iota(I32, shape, dim)


def dot(a, b):
    return jnp.dot(a, b, preferred_element_type=F32)


def dot_nt(a, b):
    return lax.dot_general(a, b, (((1,), (1,)), ((), ())), preferred_element_type=F32)


def span(ka):
    return max(ka - 1, 0), min(ka + 1, 3)


def rows(start, size):
    return pl.ds(pl.multiple_of(start, size), size)


def split3(x):
    h = x.astype(BF16).astype(F32)
    r = x - h
    m = r.astype(BF16).astype(F32)
    return h, m, r - m


def column(row):
    eye = iota((64, 64), 0) == iota((64, 64), 1)
    return jnp.sum(jnp.where(eye, row, 0.0), axis=1, keepdims=True)


def messages(rec_ref, ql_ref, send_ref):
    home, first, second = rec_ref[0:1], rec_ref[1:2], rec_ref[2:3]
    named = jnp.where(iota((DEVICES, 256), 0) == home, 1.0, 0.0)
    earlier = jnp.where(iota((256, 256), 0) < iota((256, 256), 1), 1.0, 0.0).astype(BF16)
    before = dot(named.astype(BF16), earlier)
    rank = jnp.sum(named * before, axis=0, keepdims=True).astype(I32)
    slot = iota((DEVICES, 256), 0)
    values = jnp.where(slot == rank, first + 1, jnp.where(slot == rank + CAP, second + 1, 0))
    out = dot_nt(named.astype(BF16), values.astype(F32).astype(BF16))
    box = iota((64, 128), 0)
    parent = box // 32 * 4 + box // 8 % 2 * 2 + box % 4 // 2
    charge = jnp.sum(ql_ref[...], axis=1, keepdims=True)
    mine = jnp.where(iota((64, 128), 1) == parent + 2 * CAP, charge, 0.0)
    send_ref[...] = out + jnp.sum(mine, axis=0, keepdims=True)


def planes(pos_ref, wid_ref, left_ref, right_ref):
    box = iota((64, 128), 0)
    cells = (box // 16, box // 4 % 4, box % 4)
    norm = wid_ref[...]
    one = jnp.ones((64, 128), F32)
    for c in range(3):
        x = pos_ref[c] + (cells[c].astype(F32) - 2.0)
        norm = norm + x * x
        left_ref[64 * c : 64 * c + 64] = -2.0 * x
        right_ref[64 * c : 64 * c + 64] = x
    left_ref[192:256], right_ref[192:256] = norm, one
    left_ref[256:320], right_ref[256:320] = one, norm
    left_ref[320:512] = jnp.zeros((192, 128), F32)
    right_ref[320:512] = jnp.zeros((192, 128), F32)


def features(g, left_ref, right_ref, ql_ref, lt_ref, rt_ref, qc_ref):
    eye = jnp.where(iota((128, 128), 0) == iota((128, 128), 1), 1.0, 0.0).astype(BF16)
    pad = jnp.zeros((128 - DEPTH, 128), BF16)
    packed = []
    for k in range(8):
        b = 8 * g + k
        h, m, l = split3(left_ref[pl.ds(b, 8, stride=64), :])
        packed.append(jnp.concatenate([h, h, m, m, h, l], axis=0).astype(BF16))
        h, m, l = split3(right_ref[pl.ds(b, 8, stride=64), :])
        lanes = slice(128 * (k % 4), 128 * (k % 4) + 128)
        rt_ref[2 * g + k // 4, :, lanes] = jnp.concatenate([h, m, h, m, l, h], axis=0).astype(BF16)
    for k in range(0, 8, 2):
        t = dot_nt(eye, jnp.concatenate([packed[k], pad, packed[k + 1], pad], axis=0))
        for kk in (0, 1):
            lt_ref[rows((8 * g + k + kk) * 128, 128), :] = t[:, 128 * kk : 128 * kk + DEPTH].astype(BF16)
    q = ql_ref[rows(8 * g, 8), :].T
    for k in range(8):
        qc_ref[rows((8 * g + k) * 128, 128), :] = jnp.broadcast_to(q[:, k : k + 1], (128, 128))


CROSS_SPANS = [(ka, *span(ka)) for ka in range(4)]
OWN_SPANS = [(ka, ka + 1, ka + 1) for ka in range(3)]
PAIRS = 42
TRIPLES = 2
STEPS = 14 // TRIPLES


def key_of(kind, ka, kb):
    return 32 * ka + 4 * kind + kb


def produce(r1, r2, kind, slot, spans, back, ql_ref, qc_ref, lt_ref, rt_ref, set_ref, back_ref):
    lanes = iota((128, 128), 1) - 4 * kind
    tile = None
    for ka, lo, hi in spans:
        left = lt_ref[rows(r1 * 512 + ka * 128, 128), :]
        d = dot(left, rt_ref[r2, :, lo * 128 : (hi + 1) * 128])
        kern = lax.rsqrt(d) - lax.rsqrt(d + SOFT_TERM)
        qc = qc_ref[rows(r1 * 512 + ka * 128, 128), :].reshape(16, 8, 128)
        for kb in range(lo, hi + 1):
            kk = kern[:, (kb - lo) * 128 : (kb - lo + 1) * 128]
            back_ref[back(ka, kb)] = jnp.sum(kk.reshape(16, 8, 128) * qc, axis=0)
            x = jnp.sum(kk * ql_ref[pl.ds(4 * r2 + kb, 1), :], axis=1, keepdims=True)
            tile = jnp.broadcast_to(x, (128, 128)) if tile is None else jnp.where(lanes == key_of(0, ka, kb), x, tile)
    set_ref[slot] = tile


def cross_back(slot):
    return lambda ka, kb: slot * 10 + 3 * ka - 1 * (ka > 0) + kb - span(ka)[0]


def own_back(row):
    return lambda ka, kb: PAIRS * 10 + row * 3 + ka


def step_rows(t):
    g4, g7, g10 = (t + 28) // 32, (t + 25) // 32, (t + 22) // 32
    i = t - 4 * g4 - 3 * g7 - 3 * g10
    return 4 * i + g4 - g7 - i * g10, 1 + 2 * g4 + 2 * g7 - g10, g4 + g7 + g10


def produce_own(r, refs):
    produce(r, r, 4, PAIRS + r, OWN_SPANS, own_back(r), *refs)


def produce_step(step, refs):
    for n in range(TRIPLES):
        t = TRIPLES * step + n
        base, diff, kind = step_rows(t)
        for j in range(3):
            produce(base + j, base + j + diff, kind, 3 * t + j, CROSS_SPANS, cross_back(3 * t + j), *refs)
        produce_own(t, refs)


def row_parts(i, j):
    inner = not (isinstance(i, int) and i == 3)
    parts = [(4, 0, PAIRS + 4 * i + j)]
    if j <= 2:
        parts.append((0, 1, 3 * i + j))
    if inner:
        parts.append((3, 4, 30 + 4 * i + j))
    if inner and j <= 2:
        parts.append((2, 5, 21 + 3 * i + j))
    if inner and j >= 1:
        parts.append((1, 3, 12 + 3 * i + j - 1))
    return parts


def turn_sets(set_ref, turned_ref):
    kinds = iota((128, 128), 1) % 32 // 4

    def step(i, carry):
        for j in range(4):
            tile = jnp.zeros((128, 128), F32)
            for kind, _, slot in row_parts(i, j):
                tile = jnp.where(kinds == kind, set_ref[slot], tile)
            turned_ref[4 * i + j] = tile.T
        return carry

    lax.fori_loop(0, 3, step, 0)
    step(3, 0)


def count_pairs(got, key_ref, row_ref):
    by_key, by_row = jnp.zeros((128, 128), F32), jnp.zeros((16, 128), F32)
    for k in range(CAP):
        a, b = got[k : k + 1].astype(I32) - 1, got[CAP + k : CAP + 1 + k].astype(I32) - 1
        first, second = jnp.minimum(a, b), jnp.maximum(a, b)
        r1, diff = first // 4, second // 4 - first // 4
        kind = jnp.where(diff == 0, 4, jnp.where(diff == 1, 0, jnp.where(diff == 3, 1, jnp.where(diff == 5, 2, 3))))
        key = jnp.where(first >= 0, 32 * (first % 4) + 4 * kind + second % 4, 128)
        hot_key = jnp.where(iota((128, 128), 0) == key, 1.0, 0.0).astype(BF16)
        hot_row = jnp.where(iota((16, 128), 0) == r1, 1.0, 0.0).astype(BF16)
        by_row = by_row + dot_nt(hot_row, hot_key)
        by_key = by_key + dot_nt(hot_key, jnp.concatenate([hot_row, jnp.zeros((112, 128), BF16)], axis=0))
    key_ref[...] = by_key
    for r in range(16):
        row_ref[8 * r : 8 * r + 8, :] = jnp.broadcast_to(by_row[r : r + 1], (8, 128))


def weigh(key_ref, row_ref, turned_ref, back_ref, acc_ref):
    for r in range(16):
        weighted = turned_ref[r] * jnp.broadcast_to(key_ref[:, r : r + 1], (128, 128))
        for ka in range(4):
            acc_ref[32 * r + 8 * ka : 32 * r + 8 * ka + 8, :] = jnp.sum(weighted[32 * ka : 32 * ka + 32].reshape(4, 8, 128), axis=0)

    def step(i, carry):
        for j in range(4):
            r1 = 4 * i + j
            counts = row_ref[rows(8 * r1, 8), :]
            for kind, diff, slot in row_parts(i, j):
                sums = {}
                for ka, lo, hi in OWN_SPANS if kind == 4 else CROSS_SPANS:
                    for kb in range(lo, hi + 1):
                        key = key_of(kind, ka, kb)
                        back = own_back(r1) if kind == 4 else cross_back(slot)
                        b = back_ref[back(ka, kb)] * jnp.broadcast_to(counts[:, key : key + 1], (8, 128))
                        sums[kb] = b if kb not in sums else sums[kb] + b
                for kb, b in sums.items():
                    acc_ref[rows((4 * (r1 + diff) + kb) * 8, 8), :] += b
        return carry

    lax.fori_loop(0, 3, step, 0)
    step(3, 0)


def far_field(got, u, v):
    g, src = iota((64, 128), 0), iota((64, 128), 1)
    dx0 = (4 * (u - src % GX) + g // 16).astype(F32) + 0.5
    dy0 = (4 * (v - src // GX) + g // 4 % 4).astype(F32) + 0.5
    dz0 = (g % 4).astype(F32) + 0.5
    total = jnp.zeros((64, 128), F32)
    for p in range(8):
        dx = dx0 - (2 * (p // 4) + 1)
        dy = dy0 - (2 * (p // 2 % 2) + 1)
        dz = dz0 - (2 * (p % 2) + 1)
        total = total + lax.rsqrt(dx * dx + dy * dy + dz * dz + SOFT_TERM) * got[2 * CAP + p : 2 * CAP + 1 + p]
    col = jnp.sum(total, axis=1, keepdims=True)
    eye = iota((64, 64), 0) == iota((64, 64), 1)
    return jnp.sum(jnp.where(eye, col, 0.0), axis=0, keepdims=True)


def collect(acc_ref, live, out_ref):
    total = jnp.zeros((64, 128), F32)
    for sub in range(8):
        part = [acc_ref[pl.ds(64 * g + sub, 8, stride=8), :] for g in range(8)]
        total = total + jnp.concatenate(part, axis=0)
    out_ref[...] = jnp.where(live, total, 0.0)


def kernel(
    q_hbm, pos_hbm, wid_hbm, cnt_hbm, rec_hbm, near_ref, far_ref, q_ref, pos_ref, wid_ref, cnt_ref, rec_ref, in_sem,
    left_ref, right_ref, lt_ref, rt_ref, ql_ref, qc_ref, set_ref, turned_ref, back_ref, key_ref, row_ref, acc_ref,
    send_ref, mid_ref, turn_ref, got_ref, send1, recv1, send2, recv2,
):
    u, v = lax.axis_index("gx"), lax.axis_index("gy")
    pairs = ((rec_hbm, rec_ref), (cnt_hbm, cnt_ref), (q_hbm, q_ref), (pos_hbm, pos_ref), (wid_hbm, wid_ref))
    inputs = [pltpu.make_async_copy(a, b, in_sem.at[s]) for s, (a, b) in enumerate(pairs)]
    for copy in inputs:
        copy.start()
    others_x = [lax.rem(u + s, GX) for s in range(1, GX)]
    others_y = [lax.rem(v + s, GY) for s in range(1, GY)]
    barrier = pltpu.get_barrier_semaphore()
    for x in others_x:
        pl.semaphore_signal(barrier, inc=1, device_id=(x, v), device_id_type=MESH)
    for y in others_y:
        pl.semaphore_signal(barrier, inc=1, device_id=(u, y), device_id_type=MESH)

    for copy in inputs[:3]:
        copy.wait()
    cnt = column(cnt_ref[...].astype(F32)).astype(I32)
    live = iota((64, 128), 1) < cnt
    ql_ref[...] = jnp.where(live, q_ref[...], 0.0)
    messages(rec_ref, ql_ref, send_ref)

    wave = 40 * (v % 4) + 48 * (v // 4)
    enter = 100 + wave + 82 * (u // 2)
    all_in = 100 + jnp.maximum(246 + wave, 264 + 82 * (u // 2)) + 150
    crossed = 1110
    ready = enter + 80
    late = all_in < ready + 100
    pairs_first = jnp.where(late, 0, jnp.clip((all_in - ready - FEATURE_TIME + STEP_TIME // 2) // STEP_TIME, 0, STEPS))
    pairs_second = jnp.clip((crossed - ready - FEATURE_TIME + STEP_TIME // 2) // STEP_TIME, pairs_first, STEPS)

    refs = (ql_ref, qc_ref, lt_ref, rt_ref, set_ref, back_ref)

    def pair_step(t, carry):
        produce_step(t, refs)
        return carry

    def make_features():
        for g in range(8):
            features(g, left_ref, right_ref, ql_ref, lt_ref, rt_ref, qc_ref)

    first = [
        pltpu.make_async_remote_copy(
            src_ref=send_ref.at[rows(x * GY, GY)],
            dst_ref=mid_ref.at[rows(u * GY, GY)],
            send_sem=send1.at[s],
            recv_sem=recv1.at[s],
            device_id=(x, v),
            device_id_type=MESH,
        )
        for s, x in enumerate(others_x)
    ]

    def send_first():
        pl.semaphore_wait(barrier, GX + GY - 2)
        for copy in first:
            copy.start()

    for copy in inputs[3:]:
        copy.wait()
    planes(pos_ref, wid_ref, left_ref, right_ref)
    mid_ref[rows(u * GY, GY), :] = send_ref[rows(u * GY, GY), :]
    pl.when(late)(send_first)
    make_features()
    lax.fori_loop(0, pairs_first, pair_step, 0)
    pl.when(jnp.logical_not(late))(send_first)
    lax.fori_loop(pairs_first, pairs_second, pair_step, 0)

    for copy in first:
        copy.wait_recv()
    for y in range(GY):
        turn_ref[y * GX : (y + 1) * GX, :] = mid_ref[pl.ds(y, GX, stride=GY), :]
    second = [
        pltpu.make_async_remote_copy(
            src_ref=turn_ref.at[rows(y * GX, GX)],
            dst_ref=got_ref.at[rows(v * GX, GX)],
            send_sem=send2.at[s],
            recv_sem=recv2.at[s],
            device_id=(u, y),
            device_id_type=MESH,
        )
        for s, y in enumerate(others_y)
    ]
    for copy in second:
        copy.start()
    got_ref[rows(v * GX, GX), :] = turn_ref[rows(v * GX, GX), :]

    lax.fori_loop(pairs_second, STEPS, pair_step, 0)
    for r in (14, 15):
        produce_own(r, refs)
    turn_sets(set_ref, turned_ref)

    for copy in second:
        copy.wait_recv()
    got = got_ref[...].T
    count_pairs(got, key_ref, row_ref)
    far_ref[...] = far_field(got, u, v)
    weigh(key_ref, row_ref, turned_ref, back_ref, acc_ref)
    collect(acc_ref, live, near_ref)
    for copy in first + second:
        copy.wait_send()


def body(charges, positions, widths, site_counts, pair_records):
    vmem = pltpu.VMEM
    near, far = pl.pallas_call(
        kernel,
        out_shape=(vmem((64, 128), F32), vmem((1, 64), F32)),
        in_specs=[pl.BlockSpec(memory_space=pl.ANY)] * 5,
        out_specs=(pl.BlockSpec(memory_space=vmem),) * 2,
        scratch_shapes=[
            vmem((64, 128), F32),
            vmem((3, 64, 128), F32),
            vmem((64, 128), F32),
            vmem((1, 64), I32),
            vmem((3, 256), I32),
            pltpu.SemaphoreType.DMA((5,)),
            vmem((512, 128), F32),
            vmem((512, 128), F32),
            vmem((8192, DEPTH), BF16),
            vmem((16, DEPTH, 512), BF16),
            vmem((64, 128), F32),
            vmem((8192, 128), F32),
            vmem((PAIRS + 16, 128, 128), F32),
            vmem((16, 128, 128), F32),
            vmem((468, 8, 128), F32),
            vmem((128, 128), F32),
            vmem((128, 128), F32),
            vmem((512, 128), F32),
            vmem((DEVICES, 128), F32),
            vmem((DEVICES, 128), F32),
            vmem((DEVICES, 128), F32),
            vmem((DEVICES, 128), F32),
            pltpu.SemaphoreType.DMA((GX - 1,)),
            pltpu.SemaphoreType.DMA((GX - 1,)),
            pltpu.SemaphoreType.DMA((GY - 1,)),
            pltpu.SemaphoreType.DMA((GY - 1,)),
        ],
        compiler_params=pltpu.CompilerParams(collective_id=0, has_side_effects=True, vmem_limit_bytes=56 << 20),
    )(charges, positions.transpose(1, 0, 2), widths, site_counts.reshape(1, 64), pair_records.T)
    return near, far.reshape(64)


def solution(mesh):
    return jax.shard_map(
        body,
        mesh=mesh,
        in_specs=(
            P(("gx", "gy"), None),
            P(("gx", "gy"), None, None),
            P(("gx", "gy"), None),
            P(("gx", "gy")),
            P(("gx", "gy"), None),
        ),
        out_specs=(P(("gx", "gy"), None), P(("gx", "gy"))),
        check_vma=False,
    )
```

```python
import jax
import jax.numpy as jnp
from jax import lax
from jax.experimental import pallas as pl
from jax.experimental.pallas import tpu as pltpu
from jax.sharding import PartitionSpec as P

F32, BF16, I32 = jnp.float32, jnp.bfloat16, jnp.int32
MESH = pl.DeviceIdType.MESH
GX, GY, CAP = 8, 16, 8
DEVICES = GX * GY
DEPTH = 48
SOFT_TERM = 2.0
FEATURE_TIME, STEP_TIME = 150, 136


def iota(shape, dim):
    return lax.broadcasted_iota(I32, shape, dim)


def dot(a, b):
    return jnp.dot(a, b, preferred_element_type=F32)


def dot_nt(a, b):
    return lax.dot_general(a, b, (((1,), (1,)), ((), ())), preferred_element_type=F32)


def span(ka):
    return max(ka - 1, 0), min(ka + 1, 3)


def rows(start, size):
    return pl.ds(pl.multiple_of(start, size), size)


def split3(x):
    h = x.astype(BF16).astype(F32)
    r = x - h
    m = r.astype(BF16).astype(F32)
    return h, m, r - m


def column(row):
    eye = iota((64, 64), 0) == iota((64, 64), 1)
    return jnp.sum(jnp.where(eye, row, 0.0), axis=1, keepdims=True)


def messages(rec_ref, ql_ref, send_ref):
    home, first, second = rec_ref[0:1], rec_ref[1:2], rec_ref[2:3]
    named = jnp.where(iota((DEVICES, 256), 0) == home, 1.0, 0.0)
    earlier = jnp.where(iota((256, 256), 0) < iota((256, 256), 1), 1.0, 0.0).astype(BF16)
    before = dot(named.astype(BF16), earlier)
    rank = jnp.sum(named * before, axis=0, keepdims=True).astype(I32)
    slot = iota((DEVICES, 256), 0)
    values = jnp.where(slot == rank, first + 1, jnp.where(slot == rank + CAP, second + 1, 0))
    out = dot_nt(named.astype(BF16), values.astype(F32).astype(BF16))
    box = iota((64, 128), 0)
    parent = box // 32 * 4 + box // 8 % 2 * 2 + box % 4 // 2
    charge = jnp.sum(ql_ref[...], axis=1, keepdims=True)
    mine = jnp.where(iota((64, 128), 1) == parent + 2 * CAP, charge, 0.0)
    send_ref[...] = out + jnp.sum(mine, axis=0, keepdims=True)


def planes(pos_ref, wid_ref, left_ref, right_ref):
    box = iota((64, 128), 0)
    cells = (box // 16, box // 4 % 4, box % 4)
    norm = wid_ref[...]
    one = jnp.ones((64, 128), F32)
    for c in range(3):
        x = pos_ref[c] + (cells[c].astype(F32) - 2.0)
        norm = norm + x * x
        left_ref[64 * c : 64 * c + 64] = -2.0 * x
        right_ref[64 * c : 64 * c + 64] = x
    left_ref[192:256], right_ref[192:256] = norm, one
    left_ref[256:320], right_ref[256:320] = one, norm
    left_ref[320:512] = jnp.zeros((192, 128), F32)
    right_ref[320:512] = jnp.zeros((192, 128), F32)


def features(g, left_ref, right_ref, ql_ref, lt_ref, rt_ref, qc_ref):
    eye = jnp.where(iota((128, 128), 0) == iota((128, 128), 1), 1.0, 0.0).astype(BF16)
    pad = jnp.zeros((128 - DEPTH, 128), BF16)
    packed = []
    for k in range(8):
        b = 8 * g + k
        h, m, l = split3(left_ref[pl.ds(b, 8, stride=64), :])
        packed.append(jnp.concatenate([h, h, m, m, h, l], axis=0).astype(BF16))
        h, m, l = split3(right_ref[pl.ds(b, 8, stride=64), :])
        lanes = slice(128 * (k % 4), 128 * (k % 4) + 128)
        rt_ref[2 * g + k // 4, :, lanes] = jnp.concatenate([h, m, h, m, l, h], axis=0).astype(BF16)
    for k in range(0, 8, 2):
        t = dot_nt(eye, jnp.concatenate([packed[k], pad, packed[k + 1], pad], axis=0))
        for kk in (0, 1):
            lt_ref[rows((8 * g + k + kk) * 128, 128), :] = t[:, 128 * kk : 128 * kk + DEPTH].astype(BF16)
    q = ql_ref[rows(8 * g, 8), :].T
    for k in range(8):
        qc_ref[rows((8 * g + k) * 128, 128), :] = jnp.broadcast_to(q[:, k : k + 1], (128, 128))


CROSS_SPANS = [(ka, *span(ka)) for ka in range(4)]
OWN_SPANS = [(ka, ka + 1, ka + 1) for ka in range(3)]
PAIRS = 42
TRIPLES = 2
STEPS = 14 // TRIPLES


def key_of(kind, ka, kb):
    return 32 * ka + 4 * kind + kb


def produce(r1, r2, kind, slot, spans, back, ql_ref, qc_ref, lt_ref, rt_ref, set_ref, back_ref):
    lanes = iota((128, 128), 1) - 4 * kind
    tile = None
    for ka, lo, hi in spans:
        left = lt_ref[rows(r1 * 512 + ka * 128, 128), :]
        d = dot(left, rt_ref[r2, :, lo * 128 : (hi + 1) * 128])
        kern = lax.rsqrt(d) - lax.rsqrt(d + SOFT_TERM)
        qc = qc_ref[rows(r1 * 512 + ka * 128, 128), :].reshape(16, 8, 128)
        for kb in range(lo, hi + 1):
            kk = kern[:, (kb - lo) * 128 : (kb - lo + 1) * 128]
            back_ref[back(ka, kb)] = jnp.sum(kk.reshape(16, 8, 128) * qc, axis=0)
            x = jnp.sum(kk * ql_ref[pl.ds(4 * r2 + kb, 1), :], axis=1, keepdims=True)
            tile = jnp.broadcast_to(x, (128, 128)) if tile is None else jnp.where(lanes == key_of(0, ka, kb), x, tile)
    set_ref[slot] = tile


def cross_back(slot):
    return lambda ka, kb: slot * 10 + 3 * ka - 1 * (ka > 0) + kb - span(ka)[0]


def own_back(row):
    return lambda ka, kb: PAIRS * 10 + row * 3 + ka


def step_rows(t):
    g4, g7, g10 = (t + 28) // 32, (t + 25) // 32, (t + 22) // 32
    i = t - 4 * g4 - 3 * g7 - 3 * g10
    return 4 * i + g4 - g7 - i * g10, 1 + 2 * g4 + 2 * g7 - g10, g4 + g7 + g10


def produce_own(r, refs):
    produce(r, r, 4, PAIRS + r, OWN_SPANS, own_back(r), *refs)


def produce_step(step, refs):
    for n in range(TRIPLES):
        t = TRIPLES * step + n
        base, diff, kind = step_rows(t)
        for j in range(3):
            produce(base + j, base + j + diff, kind, 3 * t + j, CROSS_SPANS, cross_back(3 * t + j), *refs)
        produce_own(t, refs)


def row_parts(i, j):
    inner = not (isinstance(i, int) and i == 3)
    parts = [(4, 0, PAIRS + 4 * i + j)]
    if j <= 2:
        parts.append((0, 1, 3 * i + j))
    if inner:
        parts.append((3, 4, 30 + 4 * i + j))
    if inner and j <= 2:
        parts.append((2, 5, 21 + 3 * i + j))
    if inner and j >= 1:
        parts.append((1, 3, 12 + 3 * i + j - 1))
    return parts


def turn_sets(set_ref, high_ref, low_ref):
    kinds = iota((128, 128), 1) % 32 // 4

    def step(i, carry):
        for j in range(4):
            tile = jnp.zeros((128, 128), F32)
            for kind, _, slot in row_parts(i, j):
                tile = jnp.where(kinds == kind, set_ref[slot], tile)
            tile = tile.T
            high = tile.astype(BF16)
            high_ref[4 * i + j] = high
            low_ref[4 * i + j] = (tile - high.astype(F32)).astype(BF16)
        return carry

    lax.fori_loop(0, 3, step, 0)
    step(3, 0)


def count_pairs(got, row_ref):
    by_row = jnp.zeros((16, 128), F32)
    for k in range(CAP):
        a, b = got[k : k + 1].astype(I32) - 1, got[CAP + k : CAP + 1 + k].astype(I32) - 1
        first, second = jnp.minimum(a, b), jnp.maximum(a, b)
        r1, diff = first // 4, second // 4 - first // 4
        kind = jnp.where(diff == 0, 4, jnp.where(diff == 1, 0, jnp.where(diff == 3, 1, jnp.where(diff == 5, 2, 3))))
        key = jnp.where(first >= 0, 32 * (first % 4) + 4 * kind + second % 4, 128)
        hot_key = jnp.where(iota((128, 128), 0) == key, 1.0, 0.0).astype(BF16)
        hot_row = jnp.where(iota((16, 128), 0) == r1, 1.0, 0.0).astype(BF16)
        by_row = by_row + dot_nt(hot_row, hot_key)
    row_ref[...] = by_row


def weigh_second(row_ref, high_ref, low_ref, first_ref):
    row, lane = iota((16, 128), 0), iota((16, 128), 1)
    mine = lane // 32 == row % 4
    for g in range(8):
        count = jnp.concatenate([jnp.broadcast_to(row_ref[2 * g + n : 2 * g + n + 1, :], (8, 128)) for n in (0, 1)], axis=0)
        high = count.astype(BF16).astype(F32)
        weight = jnp.where(mine, jnp.where(row % 8 < 4, high, count - high), 0.0).astype(BF16)
        for n in (0, 1):
            r = 2 * g + n
            x = dot(weight, high_ref[r]) + dot(weight, low_ref[r])
            first_ref[8 * r : 8 * r + 8, :] = x[8 * n : 8 * n + 8]


def weigh_first(count_ref, back_ref, acc_ref):
    sums = {}
    for r1 in range(16):
        for kind, diff, slot in row_parts(r1 // 4, r1 % 4):
            for ka, lo, hi in OWN_SPANS if kind == 4 else CROSS_SPANS:
                for kb in range(lo, hi + 1):
                    back = own_back(r1) if kind == 4 else cross_back(slot)
                    b = back_ref[back(ka, kb)] * count_ref[r1, key_of(kind, ka, kb)]
                    box = 4 * (r1 + diff) + kb
                    sums[box] = b if box not in sums else sums[box] + b
    for box in range(64):
        acc_ref[8 * box : 8 * box + 8, :] = sums.get(box, jnp.zeros((8, 128), F32))


def far_geometry(u, v, far_ref):
    g, src = iota((64, 128), 0), iota((64, 128), 1)
    dx0 = (4 * (u - src % GX) + g // 16).astype(F32) + 0.5
    dy0 = (4 * (v - src // GX) + g // 4 % 4).astype(F32) + 0.5
    dz0 = (g % 4).astype(F32) + 0.5
    for p in range(8):
        dx = dx0 - (2 * (p // 4) + 1)
        dy = dy0 - (2 * (p // 2 % 2) + 1)
        dz = dz0 - (2 * (p % 2) + 1)
        far_ref[p] = lax.rsqrt(dx * dx + dy * dy + dz * dz + SOFT_TERM)


def far_field(got, distance_ref):
    total = jnp.zeros((64, 128), F32)
    for p in range(8):
        total = total + distance_ref[p] * got[2 * CAP + p : 2 * CAP + 1 + p]
    col = jnp.sum(total, axis=1, keepdims=True)
    eye = iota((64, 64), 0) == iota((64, 64), 1)
    return jnp.sum(jnp.where(eye, col, 0.0), axis=0, keepdims=True)


def collect(acc_ref, first_ref, live, out_ref):
    total = []
    for g in range(8):
        x = [first_ref[16 * g + n : 16 * g + n + 4, :] + first_ref[16 * g + n + 4 : 16 * g + n + 8, :] for n in (0, 8)]
        part = jnp.concatenate(x, axis=0)
        for sub in range(8):
            part = part + acc_ref[pl.ds(64 * g + sub, 8, stride=8), :]
        total.append(part)
    out_ref[...] = jnp.where(live, jnp.concatenate(total, axis=0), 0.0)


def kernel(
    q_hbm, pos_hbm, wid_hbm, cnt_hbm, rec_hbm, near_ref, far_ref, q_ref, pos_ref, wid_ref, cnt_ref, rec_ref, in_sem,
    left_ref, right_ref, lt_ref, rt_ref, ql_ref, qc_ref, set_ref, high_ref, low_ref, back_ref, row_ref, count_ref, first_ref, distance_ref, acc_ref, count_sem,
    send_ref, mid_ref, turn_ref, got_ref, send1, recv1, send2, recv2,
):
    u, v = lax.axis_index("gx"), lax.axis_index("gy")
    pairs = ((rec_hbm, rec_ref), (cnt_hbm, cnt_ref), (q_hbm, q_ref), (pos_hbm, pos_ref), (wid_hbm, wid_ref))
    inputs = [pltpu.make_async_copy(a, b, in_sem.at[s]) for s, (a, b) in enumerate(pairs)]
    for copy in inputs:
        copy.start()
    others_x = [lax.rem(u + s, GX) for s in range(1, GX)]
    others_y = [lax.rem(v + s, GY) for s in range(1, GY)]
    barrier = pltpu.get_barrier_semaphore()
    for x in others_x:
        pl.semaphore_signal(barrier, inc=1, device_id=(x, v), device_id_type=MESH)
    for y in others_y:
        pl.semaphore_signal(barrier, inc=1, device_id=(u, y), device_id_type=MESH)

    for copy in inputs[:3]:
        copy.wait()
    cnt = column(cnt_ref[...].astype(F32)).astype(I32)
    live = iota((64, 128), 1) < cnt
    ql_ref[...] = jnp.where(live, q_ref[...], 0.0)
    messages(rec_ref, ql_ref, send_ref)

    wave = 40 * (v % 4) + 48 * (v // 4)
    enter = 100 + wave + 82 * (u // 2)
    all_in = 100 + jnp.maximum(246 + wave, 264 + 82 * (u // 2)) + 180
    crossed = 1150
    ready = enter + 80
    late = all_in < ready + 100
    pairs_first = jnp.where(late, 0, jnp.clip((all_in - ready - FEATURE_TIME) // STEP_TIME, 0, STEPS))
    pairs_second = jnp.clip((crossed - ready - FEATURE_TIME) // STEP_TIME, pairs_first, STEPS)

    refs = (ql_ref, qc_ref, lt_ref, rt_ref, set_ref, back_ref)

    def pair_step(t, carry):
        produce_step(t, refs)
        return carry

    def make_features():
        for g in range(8):
            features(g, left_ref, right_ref, ql_ref, lt_ref, rt_ref, qc_ref)

    first = [
        pltpu.make_async_remote_copy(
            src_ref=send_ref.at[rows(x * GY, GY)],
            dst_ref=mid_ref.at[rows(u * GY, GY)],
            send_sem=send1.at[s],
            recv_sem=recv1.at[s],
            device_id=(x, v),
            device_id_type=MESH,
        )
        for s, x in enumerate(others_x)
    ]

    def send_first():
        pl.semaphore_wait(barrier, GX + GY - 2)
        for copy in first:
            copy.start()

    for copy in inputs[3:]:
        copy.wait()
    planes(pos_ref, wid_ref, left_ref, right_ref)
    mid_ref[rows(u * GY, GY), :] = send_ref[rows(u * GY, GY), :]
    pl.when(late)(send_first)
    make_features()
    lax.fori_loop(0, pairs_first, pair_step, 0)
    pl.when(jnp.logical_not(late))(send_first)
    lax.fori_loop(pairs_first, pairs_second, pair_step, 0)

    for copy in first:
        copy.wait_recv()
    for y in range(GY):
        turn_ref[y * GX : (y + 1) * GX, :] = mid_ref[pl.ds(y, GX, stride=GY), :]
    second = [
        pltpu.make_async_remote_copy(
            src_ref=turn_ref.at[rows(y * GX, GX)],
            dst_ref=got_ref.at[rows(v * GX, GX)],
            send_sem=send2.at[s],
            recv_sem=recv2.at[s],
            device_id=(u, y),
            device_id_type=MESH,
        )
        for s, y in enumerate(others_y)
    ]
    for copy in second:
        copy.start()
    got_ref[rows(v * GX, GX), :] = turn_ref[rows(v * GX, GX), :]

    lax.fori_loop(pairs_second, STEPS, pair_step, 0)
    for r in (14, 15):
        produce_own(r, refs)
    turn_sets(set_ref, high_ref, low_ref)
    far_geometry(u, v, distance_ref)

    for copy in second:
        copy.wait_recv()
    got = got_ref[...].T
    count_pairs(got, row_ref)
    counts = pltpu.make_async_copy(row_ref, count_ref, count_sem)
    counts.start()
    weigh_second(row_ref, high_ref, low_ref, first_ref)
    far_ref[...] = far_field(got, distance_ref)
    counts.wait()
    weigh_first(count_ref, back_ref, acc_ref)
    collect(acc_ref, first_ref, live, near_ref)
    for copy in first + second:
        copy.wait_send()


def body(charges, positions, widths, site_counts, pair_records):
    vmem = pltpu.VMEM
    near, far = pl.pallas_call(
        kernel,
        out_shape=(vmem((64, 128), F32), vmem((1, 64), F32)),
        in_specs=[pl.BlockSpec(memory_space=pl.ANY)] * 5,
        out_specs=(pl.BlockSpec(memory_space=vmem),) * 2,
        scratch_shapes=[
            vmem((64, 128), F32),
            vmem((3, 64, 128), F32),
            vmem((64, 128), F32),
            vmem((1, 64), I32),
            vmem((3, 256), I32),
            pltpu.SemaphoreType.DMA((5,)),
            vmem((512, 128), F32),
            vmem((512, 128), F32),
            vmem((8192, DEPTH), BF16),
            vmem((16, DEPTH, 512), BF16),
            vmem((64, 128), F32),
            vmem((8192, 128), F32),
            vmem((PAIRS + 16, 128, 128), F32),
            vmem((16, 128, 128), BF16),
            vmem((16, 128, 128), BF16),
            vmem((468, 8, 128), F32),
            vmem((16, 128), F32),
            pltpu.SMEM((16, 128), F32),
            vmem((128, 128), F32),
            vmem((8, 64, 128), F32),
            vmem((512, 128), F32),
            pltpu.SemaphoreType.DMA,
            vmem((DEVICES, 128), F32),
            vmem((DEVICES, 128), F32),
            vmem((DEVICES, 128), F32),
            vmem((DEVICES, 128), F32),
            pltpu.SemaphoreType.DMA((GX - 1,)),
            pltpu.SemaphoreType.DMA((GX - 1,)),
            pltpu.SemaphoreType.DMA((GY - 1,)),
            pltpu.SemaphoreType.DMA((GY - 1,)),
        ],
        compiler_params=pltpu.CompilerParams(collective_id=0, has_side_effects=True, vmem_limit_bytes=56 << 20),
    )(charges, positions.transpose(1, 0, 2), widths, site_counts.reshape(1, 64), pair_records.T)
    return near, far.reshape(64)


def solution(mesh):
    return jax.shard_map(
        body,
        mesh=mesh,
        in_specs=(
            P(("gx", "gy"), None),
            P(("gx", "gy"), None, None),
            P(("gx", "gy"), None),
            P(("gx", "gy")),
            P(("gx", "gy"), None),
        ),
        out_specs=(P(("gx", "gy"), None), P(("gx", "gy"))),
        check_vma=False,
    )
```

```python
import jax
import jax.numpy as jnp
from jax import lax
from jax.experimental import pallas as pl
from jax.experimental.pallas import tpu as pltpu
from jax.sharding import PartitionSpec as P

F32, BF16, I32 = jnp.float32, jnp.bfloat16, jnp.int32
MESH = pl.DeviceIdType.MESH
GX, GY, CAP = 8, 16, 8
HEADS, HEAD_STEPS = 2, 6
DEVICES = GX * GY
DEPTH = 48
SOFT_TERM = 2.0
FEATURE_TIME, STEP_TIME = 140, 70


def iota(shape, dim):
    return lax.broadcasted_iota(I32, shape, dim)


def dot(a, b):
    return jnp.dot(a, b, preferred_element_type=F32)


def dot_nt(a, b):
    return lax.dot_general(a, b, (((1,), (1,)), ((), ())), preferred_element_type=F32)


def span(ka):
    return max(ka - 1, 0), min(ka + 1, 3)


def rows(start, size):
    return pl.ds(pl.multiple_of(start, size), size)


def split3(x):
    h = x.astype(BF16).astype(F32)
    r = x - h
    m = r.astype(BF16).astype(F32)
    return h, m, r - m


def column(row):
    eye = iota((64, 64), 0) == iota((64, 64), 1)
    return jnp.sum(jnp.where(eye, row, 0.0), axis=1, keepdims=True)


def messages(rec_ref, ql_ref, send_ref):
    home, first, second = rec_ref[0:1], rec_ref[1:2], rec_ref[2:3]
    named = jnp.where(iota((DEVICES, 256), 0) == home, 1.0, 0.0)
    earlier = jnp.where(iota((256, 256), 0) < iota((256, 256), 1), 1.0, 0.0).astype(BF16)
    before = dot(named.astype(BF16), earlier)
    rank = jnp.sum(named * before, axis=0, keepdims=True).astype(I32)
    slot = iota((DEVICES, 256), 0)
    values = jnp.where(slot == rank, first + 1, jnp.where(slot == rank + CAP, second + 1, 0))
    out = dot_nt(named.astype(BF16), values.astype(F32).astype(BF16))
    box = iota((64, 128), 0)
    parent = box // 32 * 4 + box // 8 % 2 * 2 + box % 4 // 2
    charge = jnp.sum(ql_ref[...], axis=1, keepdims=True)
    mine = jnp.where(iota((64, 128), 1) == parent + 2 * CAP, charge, 0.0)
    send_ref[...] = out + jnp.sum(mine, axis=0, keepdims=True)


def planes(pos_ref, wid_ref, left_ref, right_ref):
    box = iota((64, 128), 0)
    cells = (box // 16, box // 4 % 4, box % 4)
    norm = wid_ref[...]
    one = jnp.ones((64, 128), F32)
    for c in range(3):
        x = pos_ref[c] + (cells[c].astype(F32) - 2.0)
        norm = norm + x * x
        left_ref[64 * c : 64 * c + 64] = -2.0 * x
        right_ref[64 * c : 64 * c + 64] = x
    left_ref[192:256], right_ref[192:256] = norm, one
    left_ref[256:320], right_ref[256:320] = one, norm
    left_ref[320:512] = jnp.zeros((192, 128), F32)
    right_ref[320:512] = jnp.zeros((192, 128), F32)


def features(g, left_ref, right_ref, ql_ref, lt_ref, rt_ref, qc_ref):
    eye = jnp.where(iota((128, 128), 0) == iota((128, 128), 1), 1.0, 0.0).astype(BF16)
    pad = jnp.zeros((128 - DEPTH, 128), BF16)
    packed = []
    for k in range(8):
        b = 8 * g + k
        h, m, l = split3(left_ref[pl.ds(b, 8, stride=64), :])
        packed.append(jnp.concatenate([h, h, m, m, h, l], axis=0).astype(BF16))
        h, m, l = split3(right_ref[pl.ds(b, 8, stride=64), :])
        lanes = slice(128 * (k % 4), 128 * (k % 4) + 128)
        rt_ref[2 * g + k // 4, :, lanes] = jnp.concatenate([h, m, h, m, l, h], axis=0).astype(BF16)
    for k in range(0, 8, 2):
        t = dot_nt(eye, jnp.concatenate([packed[k], pad, packed[k + 1], pad], axis=0))
        for kk in (0, 1):
            lt_ref[rows((8 * g + k + kk) * 128, 128), :] = t[:, 128 * kk : 128 * kk + DEPTH].astype(BF16)
    q = ql_ref[rows(8 * g, 8), :].T
    for k in range(8):
        qc_ref[rows((8 * g + k) * 128, 128), :] = jnp.broadcast_to(q[:, k : k + 1], (128, 128))


CROSS_SPANS = [(ka, *span(ka)) for ka in range(4)]
OWN_SPANS = [(ka, ka + 1, ka + 1) for ka in range(3)]
PAIRS = 42
STEPS = 14


def key_of(kind, ka, kb):
    return 32 * ka + 4 * kind + kb


def produce(r1, r2, kind, slot, spans, back, ql_ref, qc_ref, lt_ref, rt_ref, set_ref, back_ref):
    lanes = iota((128, 128), 1) - 4 * kind
    tile = None
    for ka, lo, hi in spans:
        left = lt_ref[rows(r1 * 512 + ka * 128, 128), :]
        d = dot(left, rt_ref[r2, :, lo * 128 : (hi + 1) * 128])
        kern = lax.rsqrt(d) - lax.rsqrt(d + SOFT_TERM)
        qc = qc_ref[rows(r1 * 512 + ka * 128, 128), :].reshape(16, 8, 128)
        for kb in range(lo, hi + 1):
            kk = kern[:, (kb - lo) * 128 : (kb - lo + 1) * 128]
            back_ref[back(ka, kb)] = jnp.sum(kk.reshape(16, 8, 128) * qc, axis=0)
            x = jnp.sum(kk * ql_ref[pl.ds(4 * r2 + kb, 1), :], axis=1, keepdims=True)
            tile = jnp.broadcast_to(x, (128, 128)) if tile is None else jnp.where(lanes == key_of(0, ka, kb), x, tile)
    set_ref[slot] = tile


def cross_back(slot):
    return lambda ka, kb: slot * 10 + 3 * ka - 1 * (ka > 0) + kb - span(ka)[0]


def own_back(row):
    return lambda ka, kb: PAIRS * 10 + row * 3 + ka


def step_rows(t):
    g4, g7, g10 = (t + 28) // 32, (t + 25) // 32, (t + 22) // 32
    i = t - 4 * g4 - 3 * g7 - 3 * g10
    return 4 * i + g4 - g7 - i * g10, 1 + 2 * g4 + 2 * g7 - g10, g4 + g7 + g10


def produce_own(r, refs):
    produce(r, r, 4, PAIRS + r, OWN_SPANS, own_back(r), *refs)


def produce_triple(t, refs):
    base, diff, kind = step_rows(t)
    for j in range(3):
        produce(base + j, base + j + diff, kind, 3 * t + j, CROSS_SPANS, cross_back(3 * t + j), *refs)
    produce_own(t, refs)


def produce_range(start, stop, refs):
    def one(t, carry):
        produce_triple(t, refs)
        return carry

    def two(t, carry):
        produce_triple(2 * t, refs)
        produce_triple(2 * t + 1, refs)
        return carry

    lax.fori_loop(start, jnp.minimum(stop, start + start % 2), one, 0)
    lax.fori_loop((start + 1) // 2, stop // 2, two, 0)
    lax.fori_loop(jnp.maximum(stop - stop % 2, start + start % 2), stop, one, 0)


def row_parts(i, j):
    inner = not (isinstance(i, int) and i == 3)
    parts = [(4, 0, PAIRS + 4 * i + j)]
    if j <= 2:
        parts.append((0, 1, 3 * i + j))
    if inner:
        parts.append((3, 4, 30 + 4 * i + j))
    if inner and j <= 2:
        parts.append((2, 5, 21 + 3 * i + j))
    if inner and j >= 1:
        parts.append((1, 3, 12 + 3 * i + j - 1))
    return parts


def turn_sets(set_ref, high_ref, low_ref):
    kinds = iota((128, 128), 1) % 32 // 4

    def step(i, carry):
        for j in range(4):
            tile = jnp.zeros((128, 128), F32)
            for kind, _, slot in row_parts(i, j):
                tile = jnp.where(kinds == kind, set_ref[slot], tile)
            tile = tile.T
            high = tile.astype(BF16)
            high_ref[4 * i + j] = high
            low_ref[4 * i + j] = (tile - high.astype(F32)).astype(BF16)
        return carry

    lax.fori_loop(0, 3, step, 0)
    step(3, 0)


def count_pairs(got, row_ref):
    hot_row, hot_key = [], []
    for k in range(CAP):
        a, b = got[k : k + 1].astype(I32) - 1, got[CAP + k : CAP + 1 + k].astype(I32) - 1
        first, second = jnp.minimum(a, b), jnp.maximum(a, b)
        r1, diff = first // 4, second // 4 - first // 4
        kind = jnp.where(diff == 0, 4, jnp.where(diff == 1, 0, jnp.where(diff == 3, 1, jnp.where(diff == 5, 2, 3))))
        key = jnp.where(first >= 0, 32 * (first % 4) + 4 * kind + second % 4, 128)
        hot_key.append(jnp.where(iota((128, 128), 0) == key, 1.0, 0.0).astype(BF16))
        hot_row.append(jnp.where(iota((16, 128), 0) == r1, 1.0, 0.0).astype(BF16))
    row_ref[...] = dot_nt(jnp.concatenate(hot_row, axis=1), jnp.concatenate(hot_key, axis=1))


def weigh_second(row_ref, high_ref, low_ref, first_ref):
    row, lane = iota((16, 128), 0), iota((16, 128), 1)
    mine = lane // 32 == row % 4
    for g in range(8):
        count = jnp.concatenate([jnp.broadcast_to(row_ref[2 * g + n : 2 * g + n + 1, :], (8, 128)) for n in (0, 1)], axis=0)
        high = count.astype(BF16).astype(F32)
        weight = jnp.where(mine, jnp.where(row % 8 < 4, high, count - high), 0.0).astype(BF16)
        for n in (0, 1):
            r = 2 * g + n
            x = dot(weight, high_ref[r]) + dot(weight, low_ref[r])
            first_ref[8 * r : 8 * r + 8, :] = x[8 * n : 8 * n + 8]


def weigh_first(count_ref, back_ref, acc_ref):
    sums = {}
    for r1 in range(16):
        for kind, diff, slot in row_parts(r1 // 4, r1 % 4):
            for ka, lo, hi in OWN_SPANS if kind == 4 else CROSS_SPANS:
                for kb in range(lo, hi + 1):
                    back = own_back(r1) if kind == 4 else cross_back(slot)
                    b = back_ref[back(ka, kb)] * count_ref[r1, key_of(kind, ka, kb)]
                    box = 4 * (r1 + diff) + kb
                    sums[box] = b if box not in sums else sums[box] + b
    for box in range(64):
        acc_ref[8 * box : 8 * box + 8, :] = sums.get(box, jnp.zeros((8, 128), F32))


def far_geometry(u, v, far_ref):
    g, src = iota((64, 128), 0), iota((64, 128), 1)
    dx0 = (4 * (u - src % GX) + g // 16).astype(F32) + 0.5
    dy0 = (4 * (v - src // GX) + g // 4 % 4).astype(F32) + 0.5
    dz0 = (g % 4).astype(F32) + 0.5
    for p in range(8):
        dx = dx0 - (2 * (p // 4) + 1)
        dy = dy0 - (2 * (p // 2 % 2) + 1)
        dz = dz0 - (2 * (p % 2) + 1)
        far_ref[p] = lax.rsqrt(dx * dx + dy * dy + dz * dz + SOFT_TERM)


def far_field(got, distance_ref):
    total = jnp.zeros((64, 128), F32)
    for p in range(8):
        total = total + distance_ref[p] * got[2 * CAP + p : 2 * CAP + 1 + p]
    col = jnp.sum(total, axis=1, keepdims=True)
    eye = iota((64, 64), 0) == iota((64, 64), 1)
    return jnp.sum(jnp.where(eye, col, 0.0), axis=0, keepdims=True)


def collect(acc_ref, first_ref, live, out_ref):
    total = []
    for g in range(8):
        x = [first_ref[16 * g + n : 16 * g + n + 4, :] + first_ref[16 * g + n + 4 : 16 * g + n + 8, :] for n in (0, 8)]
        part = jnp.concatenate(x, axis=0)
        for sub in range(8):
            part = part + acc_ref[pl.ds(64 * g + sub, 8, stride=8), :]
        total.append(part)
    out_ref[...] = jnp.where(live, jnp.concatenate(total, axis=0), 0.0)


def kernel(
    q_hbm, pos_hbm, wid_hbm, cnt_hbm, rec_hbm, near_ref, far_ref, q_ref, pos_ref, wid_ref, cnt_ref, rec_ref, in_sem,
    left_ref, right_ref, lt_ref, rt_ref, ql_ref, qc_ref, set_ref, high_ref, low_ref, back_ref, row_ref, count_ref, first_ref, distance_ref, acc_ref, count_sem,
    send_ref, mid_ref, turn_ref, got_ref, send1, recv1, send2, recv2, head_ref, heard_ref, send3, recv3,
):
    u, v = lax.axis_index("gx"), lax.axis_index("gy")
    pairs = ((rec_hbm, rec_ref), (cnt_hbm, cnt_ref), (q_hbm, q_ref), (pos_hbm, pos_ref), (wid_hbm, wid_ref))
    inputs = [pltpu.make_async_copy(a, b, in_sem.at[s]) for s, (a, b) in enumerate(pairs)]
    for copy in inputs:
        copy.start()
    others_x = [lax.rem(u + s, GX) for s in range(1, GX)]
    others_y = [lax.rem(v + s, GY) for s in range(1, GY)]
    barrier = pltpu.get_barrier_semaphore()
    is_head = (u < HEADS) & (v == 0)
    far_heads = [(u != e) & (v != 0) for e in range(HEADS)]
    for y in others_y:
        pl.semaphore_signal(barrier, inc=1, device_id=(u, y), device_id_type=MESH)
    for x in others_x:
        pl.semaphore_signal(barrier, inc=1, device_id=(x, v), device_id_type=MESH)


    def greet_all():
        for x in others_x:
            for y in others_y:
                pl.semaphore_signal(barrier, inc=1, device_id=(x, y), device_id_type=MESH)

    pl.when(is_head)(greet_all)
    far_geometry(u, v, distance_ref)
    for copy in inputs[:3]:
        copy.wait()
    cnt = column(cnt_ref[...].astype(F32)).astype(I32)
    live = iota((64, 128), 1) < cnt
    ql_ref[...] = jnp.where(live, q_ref[...], 0.0)
    messages(rec_ref, ql_ref, send_ref)

    wave = 40 * (v % 4) + 48 * (v // 4)
    enter = 100 + wave + 82 * (u // 2) - jnp.where((u == 1) & (v == 0), 80, 0)
    all_in = 100 + jnp.maximum(246 + wave, 264 + 82 * (u // 2)) + 185
    crossed = 1110
    ready = enter + 80
    late = all_in < ready + 100
    pairs_first = jnp.where(late, 0, jnp.clip((all_in - ready - FEATURE_TIME) // STEP_TIME, 0, STEPS))
    pairs_first = jnp.where(is_head, HEAD_STEPS, pairs_first)
    pairs_second = jnp.clip((crossed - ready - FEATURE_TIME) // STEP_TIME, pairs_first, STEPS)

    refs = (ql_ref, qc_ref, lt_ref, rt_ref, set_ref, back_ref)

    def make_features():
        for g in range(8):
            features(g, left_ref, right_ref, ql_ref, lt_ref, rt_ref, qc_ref)

    first = [
        pltpu.make_async_remote_copy(
            src_ref=send_ref.at[rows(x * GY, GY)],
            dst_ref=mid_ref.at[rows(u * GY, GY)],
            send_sem=send1.at[s],
            recv_sem=recv1.at[s],
            device_id=(x, v),
            device_id_type=MESH,
        )
        for s, x in enumerate(others_x)
    ]

    to_heads = [
        pltpu.make_async_remote_copy(
            src_ref=head_ref.at[e],
            dst_ref=heard_ref.at[v * GX + u],
            send_sem=send3.at[e],
            recv_sem=recv3,
            device_id=(e, 0),
            device_id_type=MESH,
        )
        for e in range(HEADS)
    ]
    not_head = [jnp.logical_not((u == e) & (v == 0)) for e in range(HEADS)]

    def send_first():
        pl.semaphore_wait(barrier, GX + GY - 2 + sum(x.astype(I32) for x in far_heads))
        for copy in first:
            copy.start()
        for e in range(HEADS):
            pl.when(not_head[e])(to_heads[e].start)

    for copy in inputs[3:]:
        copy.wait()
    planes(pos_ref, wid_ref, left_ref, right_ref)
    mid_ref[rows(u * GY, GY), :] = send_ref[rows(u * GY, GY), :]
    for e in range(HEADS):
        head_ref[e] = send_ref[GY * e : GY * e + 1, :]
    pl.when(late)(send_first)
    make_features()
    second = [
        pltpu.make_async_remote_copy(
            src_ref=turn_ref.at[rows(y * GX, GX)],
            dst_ref=got_ref.at[rows(v * GX, GX)],
            send_sem=send2.at[s],
            recv_sem=recv2.at[s],
            device_id=(u, y),
            device_id_type=MESH,
        )
        for s, y in enumerate(others_y)
    ]
    into_head = [(u < HEADS) & (y == 0) for y in others_y]

    def pass_on():
        for copy in first:
            copy.wait_recv()
        for y in range(GY):
            turn_ref[y * GX : (y + 1) * GX, :] = mid_ref[pl.ds(y, GX, stride=GY), :]
        for copy, skip in zip(second, into_head):
            pl.when(jnp.logical_not(skip))(copy.start)
        pl.when(jnp.logical_not(is_head))(keep_own)

    def keep_own():
        got_ref[rows(v * GX, GX), :] = turn_ref[rows(v * GX, GX), :]

    def part(n, carry):
        start = jnp.where(n == 0, 0, jnp.where(n == 1, pairs_first, pairs_second))
        stop = jnp.where(n == 0, pairs_first, jnp.where(n == 1, pairs_second, STEPS))
        produce_range(start, stop, refs)
        pl.when((n == 0) & jnp.logical_not(late))(send_first)
        pl.when(n == 1)(pass_on)
        return carry

    lax.fori_loop(0, 3, part, 0)
    for r in (14, 15):
        produce_own(r, refs)
    turn_sets(set_ref, high_ref, low_ref)

    def hear():
        pltpu.make_async_copy(heard_ref.at[pl.ds(0, DEVICES - 1)], heard_ref.at[pl.ds(0, DEVICES - 1)], recv3).wait()
        own = send_ref[rows(u * GY, 8), :][0:1]
        source = iota((DEVICES, 128), 0)
        got_ref[...] = jnp.where(source == v * GX + u, own, heard_ref[:, 0, :])

    def take():
        for copy in second:
            copy.wait_recv()

    pl.when(is_head)(hear)
    pl.when(jnp.logical_not(is_head))(take)
    got = got_ref[...].T
    count_pairs(got, row_ref)
    counts = pltpu.make_async_copy(row_ref, count_ref, count_sem)
    counts.start()
    weigh_second(row_ref, high_ref, low_ref, first_ref)
    far_ref[...] = far_field(got, distance_ref)
    counts.wait()
    weigh_first(count_ref, back_ref, acc_ref)
    collect(acc_ref, first_ref, live, near_ref)
    for copy in first:
        copy.wait_send()
    for copy, skip in zip(second, into_head):
        pl.when(jnp.logical_not(skip))(copy.wait_send)
    for e in range(HEADS):
        pl.when(not_head[e])(to_heads[e].wait_send)


def body(charges, positions, widths, site_counts, pair_records):
    vmem = pltpu.VMEM
    near, far = pl.pallas_call(
        kernel,
        out_shape=(vmem((64, 128), F32), vmem((1, 64), F32)),
        in_specs=[pl.BlockSpec(memory_space=pl.ANY)] * 5,
        out_specs=(pl.BlockSpec(memory_space=vmem),) * 2,
        scratch_shapes=[
            vmem((64, 128), F32),
            vmem((3, 64, 128), F32),
            vmem((64, 128), F32),
            vmem((1, 64), I32),
            vmem((3, 256), I32),
            pltpu.SemaphoreType.DMA((5,)),
            vmem((512, 128), F32),
            vmem((512, 128), F32),
            vmem((8192, DEPTH), BF16),
            vmem((16, DEPTH, 512), BF16),
            vmem((64, 128), F32),
            vmem((8192, 128), F32),
            vmem((PAIRS + 16, 128, 128), F32),
            vmem((16, 128, 128), BF16),
            vmem((16, 128, 128), BF16),
            vmem((468, 8, 128), F32),
            vmem((16, 128), F32),
            pltpu.SMEM((16, 128), F32),
            vmem((128, 128), F32),
            vmem((8, 64, 128), F32),
            vmem((512, 128), F32),
            pltpu.SemaphoreType.DMA,
            vmem((DEVICES, 128), F32),
            vmem((DEVICES, 128), F32),
            vmem((DEVICES, 128), F32),
            vmem((DEVICES, 128), F32),
            pltpu.SemaphoreType.DMA((GX - 1,)),
            pltpu.SemaphoreType.DMA((GX - 1,)),
            pltpu.SemaphoreType.DMA((GY - 1,)),
            pltpu.SemaphoreType.DMA((GY - 1,)),
            vmem((HEADS, 1, 128), F32),
            vmem((DEVICES, 1, 128), F32),
            pltpu.SemaphoreType.DMA((HEADS,)),
            pltpu.SemaphoreType.DMA,
        ],
        compiler_params=pltpu.CompilerParams(collective_id=0, has_side_effects=True, vmem_limit_bytes=56 << 20),
    )(charges, positions.transpose(1, 0, 2), widths, site_counts.reshape(1, 64), pair_records.T)
    return near, far.reshape(64)


def solution(mesh):
    return jax.shard_map(
        body,
        mesh=mesh,
        in_specs=(
            P(("gx", "gy"), None),
            P(("gx", "gy"), None, None),
            P(("gx", "gy"), None),
            P(("gx", "gy")),
            P(("gx", "gy"), None),
        ),
        out_specs=(P(("gx", "gy"), None), P(("gx", "gy"))),
        check_vma=False,
    )
```

```python
import jax
import jax.numpy as jnp
from jax import lax
from jax.experimental import pallas as pl
from jax.experimental.pallas import tpu as pltpu
from jax.sharding import PartitionSpec as P

F32, BF16, I32 = jnp.float32, jnp.bfloat16, jnp.int32
MESH = pl.DeviceIdType.MESH
GX, GY, CAP = 8, 16, 8
HEADS, HEAD_STEPS = 2, 6
DEVICES = GX * GY
DEPTH = 48
SOFT_TERM = 2.0
FEATURE_TIME, STEP_TIME = 140, 70


def iota(shape, dim):
    return lax.broadcasted_iota(I32, shape, dim)


def dot(a, b):
    return jnp.dot(a, b, preferred_element_type=F32)


def dot_nt(a, b):
    return lax.dot_general(a, b, (((1,), (1,)), ((), ())), preferred_element_type=F32)


def span(ka):
    return max(ka - 1, 0), min(ka + 1, 3)


def rows(start, size):
    return pl.ds(pl.multiple_of(start, size), size)


def split3(x):
    h = x.astype(BF16).astype(F32)
    r = x - h
    m = r.astype(BF16).astype(F32)
    return h, m, r - m


def column(row):
    eye = iota((64, 64), 0) == iota((64, 64), 1)
    return jnp.sum(jnp.where(eye, row, 0.0), axis=1, keepdims=True)


def messages(rec_ref, ql_ref, send_ref):
    home, first, second = rec_ref[0:1], rec_ref[1:2], rec_ref[2:3]
    named = jnp.where(iota((DEVICES, 256), 0) == home, 1.0, 0.0)
    earlier = jnp.where(iota((256, 256), 0) < iota((256, 256), 1), 1.0, 0.0).astype(BF16)
    before = dot(named.astype(BF16), earlier)
    rank = jnp.sum(named * before, axis=0, keepdims=True).astype(I32)
    slot = iota((DEVICES, 256), 0)
    values = jnp.where(slot == rank, first + 1, jnp.where(slot == rank + CAP, second + 1, 0))
    out = dot_nt(named.astype(BF16), values.astype(F32).astype(BF16))
    box = iota((64, 128), 0)
    parent = box // 32 * 4 + box // 8 % 2 * 2 + box % 4 // 2
    charge = jnp.sum(ql_ref[...], axis=1, keepdims=True)
    mine = jnp.where(iota((64, 128), 1) == parent + 2 * CAP, charge, 0.0)
    send_ref[...] = out + jnp.sum(mine, axis=0, keepdims=True)


def planes(pos_ref, wid_ref, left_ref, right_ref):
    box = iota((64, 128), 0)
    cells = (box // 16, box // 4 % 4, box % 4)
    norm = wid_ref[...]
    one = jnp.ones((64, 128), F32)
    for c in range(3):
        x = pos_ref[c] + (cells[c].astype(F32) - 2.0)
        norm = norm + x * x
        left_ref[64 * c : 64 * c + 64] = -2.0 * x
        right_ref[64 * c : 64 * c + 64] = x
    left_ref[192:256], right_ref[192:256] = norm, one
    left_ref[256:320], right_ref[256:320] = one, norm
    left_ref[320:512] = jnp.zeros((192, 128), F32)
    right_ref[320:512] = jnp.zeros((192, 128), F32)


def features(g, left_ref, right_ref, ql_ref, lt_ref, rt_ref, qc_ref):
    eye = jnp.where(iota((128, 128), 0) == iota((128, 128), 1), 1.0, 0.0).astype(BF16)
    pad = jnp.zeros((128 - DEPTH, 128), BF16)
    packed = []
    for k in range(8):
        b = 8 * g + k
        h, m, l = split3(left_ref[pl.ds(b, 8, stride=64), :])
        packed.append(jnp.concatenate([h, h, m, m, h, l], axis=0).astype(BF16))
        h, m, l = split3(right_ref[pl.ds(b, 8, stride=64), :])
        lanes = slice(128 * (k % 4), 128 * (k % 4) + 128)
        rt_ref[2 * g + k // 4, :, lanes] = jnp.concatenate([h, m, h, m, l, h], axis=0).astype(BF16)
    for k in range(0, 8, 2):
        t = dot_nt(eye, jnp.concatenate([packed[k], pad, packed[k + 1], pad], axis=0))
        for kk in (0, 1):
            lt_ref[rows((8 * g + k + kk) * 128, 128), :] = t[:, 128 * kk : 128 * kk + DEPTH].astype(BF16)
    q = ql_ref[rows(8 * g, 8), :].T
    for k in range(8):
        qc_ref[rows((8 * g + k) * 128, 128), :] = jnp.broadcast_to(q[:, k : k + 1], (128, 128))


CROSS_SPANS = [(ka, *span(ka)) for ka in range(4)]
OWN_SPANS = [(ka, ka + 1, ka + 1) for ka in range(3)]
PAIRS = 42
STEPS = 14


def key_of(kind, ka, kb):
    return 32 * ka + 4 * kind + kb


def produce(r1, r2, kind, slot, spans, back, ql_ref, qc_ref, lt_ref, rt_ref, set_ref, back_ref):
    lanes = iota((128, 128), 1) - 4 * kind
    tile = None
    for ka, lo, hi in spans:
        left = lt_ref[rows(r1 * 512 + ka * 128, 128), :]
        d = dot(left, rt_ref[r2, :, lo * 128 : (hi + 1) * 128])
        kern = lax.rsqrt(d) - lax.rsqrt(d + SOFT_TERM)
        qc = qc_ref[rows(r1 * 512 + ka * 128, 128), :].reshape(16, 8, 128)
        for kb in range(lo, hi + 1):
            kk = kern[:, (kb - lo) * 128 : (kb - lo + 1) * 128]
            back_ref[back(ka, kb)] = jnp.sum(kk.reshape(16, 8, 128) * qc, axis=0)
            x = jnp.sum(kk * ql_ref[pl.ds(4 * r2 + kb, 1), :], axis=1, keepdims=True)
            tile = jnp.broadcast_to(x, (128, 128)) if tile is None else jnp.where(lanes == key_of(0, ka, kb), x, tile)
    set_ref[slot] = tile


def cross_back(slot):
    return lambda ka, kb: slot * 10 + 3 * ka - 1 * (ka > 0) + kb - span(ka)[0]


def own_back(row):
    return lambda ka, kb: PAIRS * 10 + row * 3 + ka


def step_rows(t):
    g4, g7, g10 = (t + 28) // 32, (t + 25) // 32, (t + 22) // 32
    i = t - 4 * g4 - 3 * g7 - 3 * g10
    return 4 * i + g4 - g7 - i * g10, 1 + 2 * g4 + 2 * g7 - g10, g4 + g7 + g10


def produce_own(r, refs):
    produce(r, r, 4, PAIRS + r, OWN_SPANS, own_back(r), *refs)


def produce_triple(t, refs):
    base, diff, kind = step_rows(t)
    for j in range(3):
        produce(base + j, base + j + diff, kind, 3 * t + j, CROSS_SPANS, cross_back(3 * t + j), *refs)
    produce_own(t, refs)


def produce_range(start, stop, refs):
    def one(t, carry):
        produce_triple(t, refs)
        return carry

    def three(t, carry):
        for n in range(3):
            produce_triple(3 * t + n, refs)
        return carry

    begin, end = (start + 2) // 3, stop // 3
    lax.fori_loop(start, jnp.minimum(stop, 3 * begin), one, 0)
    lax.fori_loop(begin, end, three, 0)
    lax.fori_loop(jnp.maximum(3 * end, 3 * begin), stop, one, 0)


def row_parts(i, j):
    inner = not (isinstance(i, int) and i == 3)
    parts = [(4, 0, PAIRS + 4 * i + j)]
    if j <= 2:
        parts.append((0, 1, 3 * i + j))
    if inner:
        parts.append((3, 4, 30 + 4 * i + j))
    if inner and j <= 2:
        parts.append((2, 5, 21 + 3 * i + j))
    if inner and j >= 1:
        parts.append((1, 3, 12 + 3 * i + j - 1))
    return parts


def turn_sets(set_ref, high_ref, low_ref):
    kinds = iota((128, 128), 1) % 32 // 4

    def step(i, carry):
        for j in range(4):
            tile = jnp.zeros((128, 128), F32)
            for kind, _, slot in row_parts(i, j):
                tile = jnp.where(kinds == kind, set_ref[slot], tile)
            tile = tile.T
            high = tile.astype(BF16)
            high_ref[4 * i + j] = high
            low_ref[4 * i + j] = (tile - high.astype(F32)).astype(BF16)
        return carry

    lax.fori_loop(0, 3, step, 0)
    step(3, 0)


def count_pairs(got, row_ref):
    hot_row, hot_key = [], []
    for k in range(CAP):
        a, b = got[k : k + 1].astype(I32) - 1, got[CAP + k : CAP + 1 + k].astype(I32) - 1
        first, second = jnp.minimum(a, b), jnp.maximum(a, b)
        r1, diff = first // 4, second // 4 - first // 4
        kind = jnp.where(diff == 0, 4, jnp.where(diff == 1, 0, jnp.where(diff == 3, 1, jnp.where(diff == 5, 2, 3))))
        key = jnp.where(first >= 0, 32 * (first % 4) + 4 * kind + second % 4, 128)
        hot_key.append(jnp.where(iota((128, 128), 0) == key, 1.0, 0.0).astype(BF16))
        hot_row.append(jnp.where(iota((16, 128), 0) == r1, 1.0, 0.0).astype(BF16))
    row_ref[...] = dot_nt(jnp.concatenate(hot_row, axis=1), jnp.concatenate(hot_key, axis=1))


def weigh_second(row_ref, high_ref, low_ref, first_ref):
    row, lane = iota((16, 128), 0), iota((16, 128), 1)
    mine = lane // 32 == row % 4
    for g in range(8):
        count = jnp.concatenate([jnp.broadcast_to(row_ref[2 * g + n : 2 * g + n + 1, :], (8, 128)) for n in (0, 1)], axis=0)
        high = count.astype(BF16).astype(F32)
        weight = jnp.where(mine, jnp.where(row % 8 < 4, high, count - high), 0.0).astype(BF16)
        for n in (0, 1):
            r = 2 * g + n
            x = dot(weight, high_ref[r]) + dot(weight, low_ref[r])
            first_ref[8 * r : 8 * r + 8, :] = x[8 * n : 8 * n + 8]


def weigh_first(count_ref, back_ref, acc_ref):
    sums = {}
    for r1 in range(16):
        for kind, diff, slot in row_parts(r1 // 4, r1 % 4):
            for ka, lo, hi in OWN_SPANS if kind == 4 else CROSS_SPANS:
                for kb in range(lo, hi + 1):
                    back = own_back(r1) if kind == 4 else cross_back(slot)
                    b = back_ref[back(ka, kb)] * count_ref[r1, key_of(kind, ka, kb)]
                    box = 4 * (r1 + diff) + kb
                    sums[box] = b if box not in sums else sums[box] + b
    for box in range(64):
        acc_ref[8 * box : 8 * box + 8, :] = sums.get(box, jnp.zeros((8, 128), F32))


def far_geometry(u, v, far_ref):
    g, src = iota((64, 128), 0), iota((64, 128), 1)
    dx0 = (4 * (u - src % GX) + g // 16).astype(F32) + 0.5
    dy0 = (4 * (v - src // GX) + g // 4 % 4).astype(F32) + 0.5
    dz0 = (g % 4).astype(F32) + 0.5
    for p in range(8):
        dx = dx0 - (2 * (p // 4) + 1)
        dy = dy0 - (2 * (p // 2 % 2) + 1)
        dz = dz0 - (2 * (p % 2) + 1)
        far_ref[p] = lax.rsqrt(dx * dx + dy * dy + dz * dz + SOFT_TERM)


def far_field(got, distance_ref):
    total = jnp.zeros((64, 128), F32)
    for p in range(8):
        total = total + distance_ref[p] * got[2 * CAP + p : 2 * CAP + 1 + p]
    col = jnp.sum(total, axis=1, keepdims=True)
    eye = iota((64, 64), 0) == iota((64, 64), 1)
    return jnp.sum(jnp.where(eye, col, 0.0), axis=0, keepdims=True)


def collect(acc_ref, first_ref, live, out_ref):
    total = []
    for g in range(8):
        x = [first_ref[16 * g + n : 16 * g + n + 4, :] + first_ref[16 * g + n + 4 : 16 * g + n + 8, :] for n in (0, 8)]
        part = jnp.concatenate(x, axis=0)
        for sub in range(8):
            part = part + acc_ref[pl.ds(64 * g + sub, 8, stride=8), :]
        total.append(part)
    out_ref[...] = jnp.where(live, jnp.concatenate(total, axis=0), 0.0)


def kernel(
    q_hbm, pos_hbm, wid_hbm, cnt_hbm, rec_hbm, near_ref, far_ref, q_ref, pos_ref, wid_ref, cnt_ref, rec_ref, in_sem,
    left_ref, right_ref, lt_ref, rt_ref, ql_ref, qc_ref, set_ref, high_ref, low_ref, back_ref, row_ref, count_ref, first_ref, distance_ref, acc_ref, count_sem,
    send_ref, mid_ref, turn_ref, got_ref, send1, recv1, send2, recv2, head_ref, heard_ref, send3, recv3,
):
    u, v = lax.axis_index("gx"), lax.axis_index("gy")
    pairs = ((rec_hbm, rec_ref), (cnt_hbm, cnt_ref), (q_hbm, q_ref), (pos_hbm, pos_ref), (wid_hbm, wid_ref))
    inputs = [pltpu.make_async_copy(a, b, in_sem.at[s]) for s, (a, b) in enumerate(pairs)]
    for copy in inputs:
        copy.start()
    others_x = [lax.rem(u + s, GX) for s in range(1, GX)]
    others_y = [lax.rem(v + s, GY) for s in range(1, GY)]
    barrier = pltpu.get_barrier_semaphore()
    is_head = (u < HEADS) & (v == 0)
    far_heads = [(u != e) & (v != 0) for e in range(HEADS)]
    for y in others_y:
        pl.semaphore_signal(barrier, inc=1, device_id=(u, y), device_id_type=MESH)
    for x in others_x:
        pl.semaphore_signal(barrier, inc=1, device_id=(x, v), device_id_type=MESH)


    def greet_all():
        for x in others_x:
            for y in others_y:
                pl.semaphore_signal(barrier, inc=1, device_id=(x, y), device_id_type=MESH)

    pl.when(is_head)(greet_all)
    far_geometry(u, v, distance_ref)
    for copy in inputs[:3]:
        copy.wait()
    cnt = column(cnt_ref[...].astype(F32)).astype(I32)
    live = iota((64, 128), 1) < cnt
    ql_ref[...] = jnp.where(live, q_ref[...], 0.0)
    messages(rec_ref, ql_ref, send_ref)

    wave = 40 * (v % 4) + 48 * (v // 4)
    enter = 100 + wave + 82 * (u // 2) - jnp.where((u == 1) & (v == 0), 80, 0)
    all_in = 100 + jnp.maximum(246 + wave, 264 + 82 * (u // 2)) + 185
    crossed = 1110
    ready = enter + 80
    late = all_in < ready + 100
    pairs_first = jnp.where(late, 0, jnp.clip((all_in - ready - FEATURE_TIME) // STEP_TIME, 0, STEPS))
    pairs_first = jnp.where(is_head, HEAD_STEPS, pairs_first)
    pairs_second = jnp.clip((crossed - ready - FEATURE_TIME) // STEP_TIME, pairs_first, STEPS)

    refs = (ql_ref, qc_ref, lt_ref, rt_ref, set_ref, back_ref)

    def make_features():
        for g in range(8):
            features(g, left_ref, right_ref, ql_ref, lt_ref, rt_ref, qc_ref)

    first = [
        pltpu.make_async_remote_copy(
            src_ref=send_ref.at[rows(x * GY, GY)],
            dst_ref=mid_ref.at[rows(u * GY, GY)],
            send_sem=send1.at[s],
            recv_sem=recv1.at[s],
            device_id=(x, v),
            device_id_type=MESH,
        )
        for s, x in enumerate(others_x)
    ]

    to_heads = [
        pltpu.make_async_remote_copy(
            src_ref=head_ref.at[e],
            dst_ref=heard_ref.at[v * GX + u],
            send_sem=send3.at[e],
            recv_sem=recv3,
            device_id=(e, 0),
            device_id_type=MESH,
        )
        for e in range(HEADS)
    ]
    not_head = [jnp.logical_not((u == e) & (v == 0)) for e in range(HEADS)]

    def send_first():
        pl.semaphore_wait(barrier, GX + GY - 2 + sum(x.astype(I32) for x in far_heads))
        for copy in first:
            copy.start()
        for e in range(HEADS):
            pl.when(not_head[e])(to_heads[e].start)

    for copy in inputs[3:]:
        copy.wait()
    planes(pos_ref, wid_ref, left_ref, right_ref)
    mid_ref[rows(u * GY, GY), :] = send_ref[rows(u * GY, GY), :]
    for e in range(HEADS):
        head_ref[e] = send_ref[GY * e : GY * e + 1, :]
    pl.when(late)(send_first)
    make_features()
    second = [
        pltpu.make_async_remote_copy(
            src_ref=turn_ref.at[rows(y * GX, GX)],
            dst_ref=got_ref.at[rows(v * GX, GX)],
            send_sem=send2.at[s],
            recv_sem=recv2.at[s],
            device_id=(u, y),
            device_id_type=MESH,
        )
        for s, y in enumerate(others_y)
    ]
    into_head = [(u < HEADS) & (y == 0) for y in others_y]

    def pass_on():
        for copy in first:
            copy.wait_recv()
        for y in range(GY):
            turn_ref[y * GX : (y + 1) * GX, :] = mid_ref[pl.ds(y, GX, stride=GY), :]
        for copy, skip in zip(second, into_head):
            pl.when(jnp.logical_not(skip))(copy.start)
        pl.when(jnp.logical_not(is_head))(keep_own)

    def keep_own():
        got_ref[rows(v * GX, GX), :] = turn_ref[rows(v * GX, GX), :]

    def part(n, carry):
        start = jnp.where(n == 0, 0, jnp.where(n == 1, pairs_first, pairs_second))
        stop = jnp.where(n == 0, pairs_first, jnp.where(n == 1, pairs_second, STEPS))
        produce_range(start, stop, refs)
        pl.when((n == 0) & jnp.logical_not(late))(send_first)
        pl.when(n == 1)(pass_on)
        return carry

    lax.fori_loop(0, 3, part, 0)
    for r in (14, 15):
        produce_own(r, refs)
    turn_sets(set_ref, high_ref, low_ref)

    def hear():
        pltpu.make_async_copy(heard_ref.at[pl.ds(0, DEVICES - 1)], heard_ref.at[pl.ds(0, DEVICES - 1)], recv3).wait()
        own = send_ref[rows(u * GY, 8), :][0:1]
        source = iota((DEVICES, 128), 0)
        got_ref[...] = jnp.where(source == v * GX + u, own, heard_ref[:, 0, :])

    def take():
        for copy in second:
            copy.wait_recv()

    pl.when(is_head)(hear)
    pl.when(jnp.logical_not(is_head))(take)
    got = got_ref[...].T
    count_pairs(got, row_ref)
    counts = pltpu.make_async_copy(row_ref, count_ref, count_sem)
    counts.start()
    weigh_second(row_ref, high_ref, low_ref, first_ref)
    far_ref[...] = far_field(got, distance_ref)
    counts.wait()
    weigh_first(count_ref, back_ref, acc_ref)
    collect(acc_ref, first_ref, live, near_ref)
    for copy in first:
        copy.wait_send()
    for copy, skip in zip(second, into_head):
        pl.when(jnp.logical_not(skip))(copy.wait_send)
    for e in range(HEADS):
        pl.when(not_head[e])(to_heads[e].wait_send)


def body(charges, positions, widths, site_counts, pair_records):
    vmem = pltpu.VMEM
    near, far = pl.pallas_call(
        kernel,
        out_shape=(vmem((64, 128), F32), vmem((1, 64), F32)),
        in_specs=[pl.BlockSpec(memory_space=pl.ANY)] * 5,
        out_specs=(pl.BlockSpec(memory_space=vmem),) * 2,
        scratch_shapes=[
            vmem((64, 128), F32),
            vmem((3, 64, 128), F32),
            vmem((64, 128), F32),
            vmem((1, 64), I32),
            vmem((3, 256), I32),
            pltpu.SemaphoreType.DMA((5,)),
            vmem((512, 128), F32),
            vmem((512, 128), F32),
            vmem((8192, DEPTH), BF16),
            vmem((16, DEPTH, 512), BF16),
            vmem((64, 128), F32),
            vmem((8192, 128), F32),
            vmem((PAIRS + 16, 128, 128), F32),
            vmem((16, 128, 128), BF16),
            vmem((16, 128, 128), BF16),
            vmem((468, 8, 128), F32),
            vmem((16, 128), F32),
            pltpu.SMEM((16, 128), F32),
            vmem((128, 128), F32),
            vmem((8, 64, 128), F32),
            vmem((512, 128), F32),
            pltpu.SemaphoreType.DMA,
            vmem((DEVICES, 128), F32),
            vmem((DEVICES, 128), F32),
            vmem((DEVICES, 128), F32),
            vmem((DEVICES, 128), F32),
            pltpu.SemaphoreType.DMA((GX - 1,)),
            pltpu.SemaphoreType.DMA((GX - 1,)),
            pltpu.SemaphoreType.DMA((GY - 1,)),
            pltpu.SemaphoreType.DMA((GY - 1,)),
            vmem((HEADS, 1, 128), F32),
            vmem((DEVICES, 1, 128), F32),
            pltpu.SemaphoreType.DMA((HEADS,)),
            pltpu.SemaphoreType.DMA,
        ],
        compiler_params=pltpu.CompilerParams(collective_id=0, has_side_effects=True, vmem_limit_bytes=56 << 20),
    )(charges, positions.transpose(1, 0, 2), widths, site_counts.reshape(1, 64), pair_records.T)
    return near, far.reshape(64)


def solution(mesh):
    return jax.shard_map(
        body,
        mesh=mesh,
        in_specs=(
            P(("gx", "gy"), None),
            P(("gx", "gy"), None, None),
            P(("gx", "gy"), None),
            P(("gx", "gy")),
            P(("gx", "gy"), None),
        ),
        out_specs=(P(("gx", "gy"), None), P(("gx", "gy"))),
        check_vma=False,
    )
```
